128 devices in a mesh: row: 8 (over y, core), col: 16 (over x, z).
Axes of the slice: x: 4, y: 4, z: 4, core: 2. Of those that a mesh axis runs over, the one named last changes fastest.
Arguments:
- tokens: bfloat16 [256, 768, 512], P('row', 'col'), may hold values from -6 to 6
- cloud_mask: int32 [16, 48], P('row', 'col'), may hold values from 0 to 1, as said below
- w_qkv: bfloat16 [2, 512, 1536], replicated, may hold values from -1 to 1
- b_qkv: float32 [2, 1536], replicated, may hold values from -2 to 2
- w_proj: bfloat16 [2, 512, 512], replicated, may hold values from -0.25 to 0.25
- b_proj: float32 [2, 512], replicated, may hold values from -3 to 3
- w_up: bfloat16 [2, 512, 2048], replicated, may hold values from -0.25 to 0.25
- b_up: float32 [2, 2048], replicated, may hold values from -3 to 3
- w_down: bfloat16 [2, 2048, 512], replicated, may hold values from -0.125 to 0.125
- b_down: float32 [2, 512], replicated, may hold values from -3 to 3
- norm_gain: float32 [2, 2, 512], replicated, may hold values from 0.5 to 1.5
- norm_shift: float32 [2, 2, 512], replicated, may hold values from -2 to 2
- logit_scale: float32 [2, 16], replicated, may hold values from 4 to 40
- position_table: float32 [2, 16, 961], replicated, may hold values from 0 to 16
Outputs:
- encoded: bfloat16 [256, 768, 512], P('row', 'col')
The draws below stay inside these ranges and needn't reach their ends.
Inputs may be any that keep to these rules, and one draw needn't show every extreme that they name: `cloud_mask`: the windows of each row of tiles (2 window rows across the whole image) include exactly 48 clear ones.
All inputs are finite; a program needn't handle non-finite values.
Results may differ from the reference program's by a relative error of at most 0.015.
Values may be sent and summed in bfloat16 or wider, within the bound.
A program may use at most 256 MiB of HBM per device.

```python
import math
import jax
import jax.numpy as jnp
from jax import lax

DIM = 512
HEADS = 16
HEAD_DIM = 32
FF = 2048
WIN = 16
SHIFT = 8
POS = 961
WH = 2
WW = 3
CAP = 3
IMAGE_H = 256
IMAGE_W = 768
N_ROW = 8
N_COL = 16


def draw_cloud_mask(key, part):
    key = jax.random.fold_in(key, 5)
    per_tile = WH * WW
    clear_count = CAP * N_COL
    weight_key, full_key, jitter_key = jax.random.split(key, 3)
    weight = jax.random.randint(weight_key, (N_ROW, N_COL), 0, 4)
    full_tile = jax.random.randint(full_key, (N_ROW, 1), 0, N_COL)
    weight = jnp.where(jnp.arange(N_COL)[None, :] == full_tile, 8, weight)
    jitter = jax.random.randint(jitter_key, (N_ROW, N_COL, per_tile), 0, 4096)
    serial = jnp.arange(N_COL * per_tile, dtype=jnp.int32).reshape(1, N_COL, per_tile)
    scores = (weight[:, :, None] * 4096 + jitter) * (N_COL * per_tile) + serial
    ranked = jnp.argsort(-scores.reshape(N_ROW, N_COL * per_tile), axis=1)
    position = jnp.argsort(ranked, axis=1)
    clear_flag = (position < clear_count).astype(jnp.int32).reshape(N_ROW, N_COL, WH, WW)
    return clear_flag.transpose(0, 2, 1, 3).reshape(N_ROW * WH, N_COL * WW)


def column_scales(key):
    lowest = math.log(0.06)
    highest = math.log(1.2)
    head_scale = jnp.exp(jax.random.uniform(key, (2, 2, HEADS), jnp.float32, lowest, highest))
    joined = jnp.concatenate([head_scale, jnp.ones((2, 1, HEADS), jnp.float32)], axis=1)
    return jnp.broadcast_to(joined[:, :, :, None], (2, 3, HEADS, HEAD_DIM)).reshape(2, 3 * DIM)


def draw_w_qkv(key, part):
    columns = column_scales(key)
    key = jax.random.fold_in(key, 7)
    base = jnp.clip(jax.random.normal(key, (2, DIM, 3 * DIM), jnp.float32), -4.0, 4.0)
    return (base * DIM ** (-0.5) * columns[:, None, :]).astype(jnp.bfloat16)


def draw_b_qkv(key, part):
    columns = column_scales(key)
    key = jax.random.fold_in(key, 9)
    base = 0.5 * jnp.clip(jax.random.normal(key, (2, 3 * DIM), jnp.float32), -3.0, 3.0)
    return (base * columns).astype(jnp.float32)


def levels(key, shape, cuts, smallest, top_value):
    def one(dim, shards_of):
        steps = jax.random.uniform(jax.random.fold_in(jax.random.fold_in(key, 6), dim), (shards_of,), jnp.float32, smallest / len(cuts), top_value / len(cuts))
        return jnp.repeat(jnp.exp(steps), shape[dim] // shards_of).reshape((-1,) + (1,) * (len(shape) - dim - 1))

    factor_of = one(*cuts[0])
    for cut in cuts[1:]:
        factor_of = factor_of * one(*cut)
    return factor_of


def scatter_about(stream_key, dims, scale, limit, cuts=(), kind=jnp.bfloat16):
    values = jax.random.normal(stream_key, dims, jnp.float32) * scale
    if len(cuts) > 0:
        values = levels(stream_key, dims, cuts, -0.22, 0.18) * values
    return jnp.clip(values, min=-limit, max=limit).astype(kind)


def setup_inputs(seed: int = 0) -> dict:
    key_list = jax.random.split(jax.random.key(seed), 15)
    return {
        "tokens": scatter_about(key_list[0], (IMAGE_H, IMAGE_W, DIM), 1.0, 6.0, ((0, 8), (1, 16))),
        "cloud_mask": draw_cloud_mask(jax.random.fold_in(key_list[14], 71), 0),
        "w_qkv": draw_w_qkv(jax.random.fold_in(key_list[14], 71), 0),
        "b_qkv": draw_b_qkv(jax.random.fold_in(key_list[14], 71), 0),
        "w_proj": scatter_about(key_list[4], (2, DIM, DIM), DIM ** -0.5, 0.25),
        "b_proj": scatter_about(key_list[5], (2, DIM), 0.5, 3.0, (), jnp.float32),
        "w_up": scatter_about(key_list[6], (2, DIM, FF), DIM ** -0.5, 0.25),
        "b_up": scatter_about(key_list[7], (2, FF), 0.5, 3.0, (), jnp.float32),
        "w_down": scatter_about(key_list[8], (2, FF, DIM), FF ** -0.5, 0.125),
        "b_down": scatter_about(key_list[9], (2, DIM), 0.5, 3.0, (), jnp.float32),
        "norm_gain": jnp.clip(1.0 + 0.1 * jax.random.normal(key_list[10], (2, 2, DIM), jnp.float32), 0.5, 1.5),
        "norm_shift": scatter_about(key_list[11], (2, 2, DIM), 0.3, 2.0, (), jnp.float32),
        "logit_scale": jnp.clip(jnp.exp(jax.random.uniform(key_list[12], (2, HEADS), jnp.float32, math.log(4.0), math.log(40.0))), 4.0, 40.0),
        "position_table": jnp.clip(jax.random.uniform(key_list[13], (2, HEADS, POS), jnp.float32, 0.0, 16.0), 0.0, 16.0),
    }


NORM_EPS = 1e-05

def layer_norm(values, norm_gain, norm_shift):
    average = lax.optimization_barrier(jnp.mean(values, axis=-1, keepdims=True))
    centred = values - average
    variance = lax.optimization_barrier(jnp.mean(centred * centred, axis=-1, keepdims=True))
    return centred * lax.rsqrt(variance + NORM_EPS) * norm_gain + norm_shift

def relative_bias(table):
    places = jnp.arange(WIN * WIN, dtype=jnp.int32)
    row_pos = places // WIN
    col_pos = places % WIN
    row_step = row_pos[:, None] - row_pos[None, :] + (WIN - 1)
    col_step = col_pos[:, None] - col_pos[None, :] + (WIN - 1)
    return jnp.take(table, (row_step * (2 * WIN - 1) + col_step).astype(jnp.int32), axis=1)

def to_windows(token_grid):
    rows_span, cols_span = (token_grid.shape[0], token_grid.shape[1])
    trailing = token_grid.shape[2:]
    blocked = token_grid.reshape((rows_span // WIN, WIN, cols_span // WIN, WIN) + trailing)
    axes_order = (0, 2, 1, 3) + tuple(range(4, 4 + len(trailing)))
    return blocked.transpose(axes_order).reshape((rows_span // WIN * (cols_span // WIN), WIN * WIN) + trailing)

def from_windows(blocks, rows_span, cols_span):
    trailing = blocks.shape[2:]
    blocked = blocks.reshape((rows_span // WIN, cols_span // WIN, WIN, WIN) + trailing)
    axes_order = (0, 2, 1, 3) + tuple(range(4, 4 + len(trailing)))
    return blocked.transpose(axes_order).reshape((rows_span, cols_span) + trailing)

def wrap_labels(first_row, first_col, rows_span, cols_span, image_rows, image_cols):
    row_place = (first_row + jnp.arange(rows_span, dtype=jnp.int32)) % image_rows
    col_place = (first_col + jnp.arange(cols_span, dtype=jnp.int32)) % image_cols
    return (2 * (row_place < SHIFT).astype(jnp.int32))[:, None] + (col_place < SHIFT).astype(jnp.int32)[None, :]

def unit_rows(part):
    widened = part.astype(jnp.float32)
    length = jnp.sqrt(lax.optimization_barrier(jnp.sum(widened * widened, axis=-1, keepdims=True)))
    return (widened / jnp.maximum(length, 1.0)).astype(jnp.bfloat16)

def window_block(block, label_row, layer_id, params, pos_bias):
    w_qkv, b_qkv, w_proj, b_proj, w_up, b_up, w_down, b_down, norm_gain, norm_shift, logit_scale = params
    packed = (jnp.dot(block, w_qkv[layer_id], preferred_element_type=jnp.float32) + b_qkv[layer_id]).astype(jnp.bfloat16)
    packed = packed.reshape(WIN * WIN, 3, HEADS, HEAD_DIM)
    queries = unit_rows(packed[:, 0])
    keyed = unit_rows(packed[:, 1])
    values = packed[:, 2]
    scores = jnp.einsum('qhd,khd->hqk', queries.astype(jnp.float32), keyed.astype(jnp.float32))
    scores = scores * logit_scale[layer_id][:, None, None] + pos_bias
    allowed = label_row[:, None] == label_row[None, :]
    raised = jnp.where(allowed[None], jnp.exp(scores), 0.0)
    weights = (raised / lax.optimization_barrier(jnp.sum(raised, axis=-1, keepdims=True))).astype(jnp.bfloat16)
    context = jnp.einsum('hqk,khd->qhd', weights.astype(jnp.float32), values.astype(jnp.float32)).astype(jnp.bfloat16)
    attended = jnp.dot(context.reshape(WIN * WIN, DIM), w_proj[layer_id], preferred_element_type=jnp.float32) + b_proj[layer_id]
    middle = (block.astype(jnp.float32) + layer_norm(attended, norm_gain[layer_id, 0], norm_shift[layer_id, 0])).astype(jnp.bfloat16)
    expanded = jax.nn.gelu(jnp.dot(middle, w_up[layer_id], preferred_element_type=jnp.float32) + b_up[layer_id], approximate=False).astype(jnp.bfloat16)
    reduced = jnp.dot(expanded, w_down[layer_id], preferred_element_type=jnp.float32) + b_down[layer_id]
    return (middle.astype(jnp.float32) + layer_norm(reduced, norm_gain[layer_id, 1], norm_shift[layer_id, 1])).astype(jnp.bfloat16)

def swin_block(blocks, labels, layer_id, params, position_table):
    pos_bias = relative_bias(position_table[layer_id])

    def per_window(item):
        return window_block(item[0], item[1], layer_id, params, pos_bias)
    return lax.map(per_window, (blocks, labels))

def reference(tokens, cloud_mask, w_qkv, b_qkv, w_proj, b_proj, w_up, b_up, w_down, b_down, norm_gain, norm_shift, logit_scale, position_table):
    params = (w_qkv, b_qkv, w_proj, b_proj, w_up, b_up, w_down, b_down, norm_gain, norm_shift, logit_scale)
    blocks = to_windows(tokens)
    picked = jnp.nonzero(cloud_mask.reshape(-1) == 1, size=CAP * N_COL * N_ROW)[0].astype(jnp.int32)
    chosen = blocks[picked]
    plain_labels = jnp.zeros((chosen.shape[0], WIN * WIN), jnp.int32)
    processed = swin_block(chosen, plain_labels, 0, params, position_table)
    after_first = blocks.at[picked].set(processed)
    token_grid = from_windows(after_first, IMAGE_H, IMAGE_W)
    rolled = jnp.roll(token_grid, (-SHIFT, -SHIFT), axis=(0, 1))
    labels = to_windows(wrap_labels(SHIFT, SHIFT, IMAGE_H, IMAGE_W, IMAGE_H, IMAGE_W))
    second = swin_block(to_windows(rolled), labels, 1, params, position_table)
    return jnp.roll(from_windows(second, IMAGE_H, IMAGE_W), (SHIFT, SHIFT), axis=(0, 1))
```

```python
import functools

import jax
import jax.numpy as jnp
from jax import lax
from jax.experimental import pallas as pl
from jax.experimental.pallas import tpu as pltpu
from jax.sharding import PartitionSpec as P

DIM = 512
HEADS = 16
HEAD_DIM = 32
FF = 2048
WIN = 16
HALF = 8
SPAN = 31
POS = 961
TOK = WIN * WIN
NORM_EPS = 1e-05
LOG2E = 1.4426950408889634
LANES_POS = 1024

GELU_POLY = (
    0.7978842161310574,
    0.03633428346473718,
    -3.312995621886861e-05,
    -5.52401697057975e-05,
    3.969110988768427e-06,
    -1.3344650342438986e-07,
    1.8056185099931046e-09,
)
GELU_CAP = 32.0

F32 = jnp.float32
BF16 = jnp.bfloat16
MESH = pl.DeviceIdType.MESH


def dot(a, b):
    return jnp.dot(a, b, preferred_element_type=F32)


def gelu(x):
    u = jnp.minimum(x * x, GELU_CAP)
    p = GELU_POLY[-1]
    for c in GELU_POLY[-2::-1]:
        p = p * u + c
    h = 0.5 * x
    return h * jnp.tanh(x * p) + h


def layer_norm(v, g, s):
    m = jnp.mean(v, axis=-1, keepdims=True)
    c = v - m
    var = jnp.mean(c * c, axis=-1, keepdims=True)
    return c * lax.rsqrt(var + NORM_EPS) * g + s


def build_bias(table, tscr, wscr, bias):
    tscr[...] = jnp.zeros_like(tscr)
    for b in range(2):
        tscr[b * HEADS : (b + 1) * HEADS, 0:POS] = table[b] * LOG2E
    rows = lax.broadcasted_iota(jnp.int32, (LANES_POS, 256), 0)
    lane = lax.broadcasted_iota(jnp.int32, (1, 256), 1)
    target = (30 - (lane >> 3)) * SPAN + 7 - (lane & 7)
    pick = jnp.where(rows == target, 1.0, 0.0).astype(BF16)
    for d in range(3):
        t = tscr[...]
        rolled = [
            pltpu.roll(t, LANES_POS - (8 * d + c), 1) if 8 * d + c else t for c in range(8)
        ]
        r = jnp.concatenate(rolled, axis=0)
        hi = r.astype(BF16)
        r = r - hi.astype(F32)
        mid = r.astype(BF16)
        lo = (r - mid.astype(F32)).astype(BF16)
        w = dot(hi, pick) + dot(mid, pick) + dot(lo, pick)
        for half in range(2):
            wscr[half, d * 256 : (d + 1) * 256, :] = w[:, half * 128 : (half + 1) * 128]

    def expand(bh, carry):
        b = bh // HEADS
        h = bh % HEADS
        for d in range(3):
            rows8 = pl.ds(d * 256 + bh, 8, stride=32)
            w = jnp.concatenate([wscr[0, rows8, :], wscr[1, rows8, :]], axis=1)
            for rp in range(WIN):
                o = (15 - rp) * 8
                piece = w[:, o : o + 128]
                for bp in range(2):
                    bq = bp - (d - 1)
                    if 0 <= bq < 2:
                        bias[b, h, bp * 128 + rp * 8 : bp * 128 + rp * 8 + 8, bq * 128 : bq * 128 + 128] = piece
        return carry

    lax.fori_loop(0, 2 * HEADS, expand, 0)


def kernel(
    remote,
    tok_hbm, mask, wqkv_hbm, bqkv, wproj_hbm, bproj, wup_hbm, bup, wdown_hbm, bdown,
    gain, shift, lscale, table,
    out,
    tok, wqkv, wproj, wup, wdown, buf, bias, tscr, wscr, prob, vone, ctx, hid, same, load_sem, send_sem, recv_sem,
):
    tile_rows, tile_cols = tok.shape[0], tok.shape[1]
    wh, ww = tile_rows // WIN, tile_cols // WIN
    nwin = wh * ww
    own = tile_rows * HALF
    edge_rows = HALF * HALF
    halves = 2 * ww

    loads = [
        pltpu.make_async_copy(tok_hbm, tok, load_sem.at[0]),
        pltpu.make_async_copy(wqkv_hbm, wqkv, load_sem.at[1]),
        pltpu.make_async_copy(wproj_hbm, wproj, load_sem.at[2]),
        pltpu.make_async_copy(wup_hbm, wup, load_sem.at[3]),
        pltpu.make_async_copy(wdown_hbm, wdown, load_sem.at[4]),
    ]
    for c in loads:
        c.start()

    if remote:
        row, col = lax.axis_index("row"), lax.axis_index("col")
        nrow, ncol = lax.axis_size("row"), lax.axis_size("col")
        up, down = lax.rem(row + nrow - 1, nrow), lax.rem(row + 1, nrow)
        left, right = lax.rem(col + ncol - 1, ncol), lax.rem(col + 1, ncol)
        barrier = pltpu.get_barrier_semaphore()
        for dev in ((up, col), (row, left), (up, left), (down, col), (row, right), (down, right)):
            pl.semaphore_signal(barrier, inc=1, device_id=dev, device_id_type=MESH)
        pl.semaphore_wait(barrier, 6)
        last_row = row == nrow - 1
        last_col = col == ncol - 1

        def copy(k, src, dst, dev):
            return pltpu.make_async_remote_copy(
                src_ref=src, dst_ref=dst, send_sem=send_sem.at[k], recv_sem=recv_sem.at[k],
                device_id=dev, device_id_type=MESH,
            )

        first, second = buf.at[1], buf.at[2]
        inner = pl.ds(0, edge_rows)
        outer = pl.ds(own, edge_rows)
        halo = [
            copy(0, first.at[pl.ds(0, halves), inner], first.at[pl.ds(0, halves), outer], (up, col)),
            copy(1, first.at[0, pl.ds(0, own)], first.at[halves, pl.ds(0, own)], (row, left)),
            copy(2, first.at[0, inner], first.at[halves, outer], (up, left)),
        ]
        back = [[] for _ in range(nwin)]
        k = 3
        for i in range(wh):
            for j in range(ww):
                n = i * ww + j
                low, right_edge = i == wh - 1, j == ww - 1
                start = edge_rows + i * TOK // 2
                size = TOK // 2 - (edge_rows if low else 0)
                if low:
                    cnt = 1 if right_edge else 2
                    cols = pl.ds(2 * j + 1, cnt)
                    back[n].append(copy(k, second.at[cols, outer], second.at[cols, inner], (down, col)))
                    k += 1
                if right_edge:
                    rows = pl.ds(start, size)
                    back[n].append(copy(k, second.at[halves, rows], second.at[0, rows], (row, right)))
                    k += 1
                if low and right_edge:
                    back[n].append(copy(k, second.at[halves, outer], second.at[0, inner], (down, right)))
                    k += 1
    else:
        last_row = last_col = jnp.bool_(False)

    build_bias(table, tscr, wscr, bias)

    r256 = lax.broadcasted_iota(jnp.int32, (256, 256), 0)
    c256 = lax.broadcasted_iota(jnp.int32, (256, 256), 1)
    same[...] = jnp.where((r256 >> 5) == (c256 >> 5), 1.0, 0.0).astype(BF16)
    lane128 = lax.broadcasted_iota(jnp.int32, (TOK, 128), 1)
    for h in range(4):
        vone[h * TOK : (h + 1) * TOK, 128:256] = jnp.where((lane128 >> 5) == h, 1.0, 0.0).astype(BF16)

    loads[0].wait()
    for j in range(ww):
        t = tok[:, j * WIN : (j + 1) * WIN, :].astype(F32)
        for b in range(2):
            buf[0, 2 * j + b, 0:own, :] = t[:, b * HALF : (b + 1) * HALF, :].reshape(own, DIM).astype(BF16)
    for c in loads[1:]:
        c.wait()

    lane256 = lax.broadcasted_iota(jnp.int32, (TOK, 256), 1)
    lane512 = lax.broadcasted_iota(jnp.int32, (1, DIM), 1)

    def window(w, carry):
        b = w // nwin
        n = w % nwin
        idx = n + b * (nwin - 1 - 2 * n)
        i = idx // ww
        j = idx % ww
        if remote:
            @pl.when(w == nwin)
            def _():
                for c in halo:
                    c.wait_recv()

        cb = 2 * j + b
        r0 = pl.multiple_of(i * (TOK // 2) + b * edge_rows, edge_rows)
        half_rows = pl.ds(r0, TOK // 2)
        x = jnp.concatenate([buf[b, cb, half_rows, :], buf[b, cb + 1, half_rows, :]], axis=0)

        q = dot(x, wqkv[b, :, 0:DIM]) + bqkv[pl.ds(b, 1), 0:DIM]
        k_ = dot(x, wqkv[b, :, DIM : 2 * DIM]) + bqkv[pl.ds(b, 1), DIM : 2 * DIM]
        v = (dot(x, wqkv[b, :, 2 * DIM : 3 * DIM]) + bqkv[pl.ds(b, 1), 2 * DIM : 3 * DIM]).astype(BF16)
        sc = jnp.zeros((1, DIM), F32)
        for h in range(HEADS):
            sc = jnp.where((lane512 >> 5) == h, lscale[b, h] * LOG2E, sc)

        r2 = lax.broadcasted_iota(jnp.int32, (TOK, TOK), 0)
        c2 = lax.broadcasted_iota(jnp.int32, (TOK, TOK), 1)
        cut_row = jnp.logical_and(jnp.logical_and(last_row, b == 1), i == wh - 1)
        cut_col = jnp.logical_and(jnp.logical_and(last_col, b == 1), j == ww - 1)
        cut = cut_row.astype(jnp.int32) * edge_rows + cut_col.astype(jnp.int32) * (TOK // 2)
        allowed = jnp.where(((r2 ^ c2) & cut) == 0, 1.0, 0.0).astype(BF16)

        for g in range(2):
            lanes = slice(g * 256, (g + 1) * 256)
            qg, kg = q[:, lanes], k_[:, lanes]
            q2 = dot((qg * qg).astype(BF16), same[...])
            k2 = dot((kg * kg).astype(BF16), same[...])
            qn = (qg * lax.rsqrt(jnp.maximum(q2, 1.0)) * sc[:, lanes]).astype(BF16)
            kn = (kg * lax.rsqrt(jnp.maximum(k2, 1.0))).astype(BF16)
            for gg in range(2):
                v0 = g * 256 + gg * 128
                vg = v[:, v0 : v0 + 128]
                for h in range(4):
                    vone[h * TOK : (h + 1) * TOK, 0:128] = jnp.where(
                        (lane128 >> 5) == h, vg, jnp.zeros_like(vg)
                    )
                    hh = gg * 4 + h
                    qm = jnp.where((lane256 >> 5) == hh, qn, jnp.zeros_like(qn))
                    s = lax.dot_general(
                        qm, kn, (((1,), (1,)), ((), ())), preferred_element_type=F32
                    )
                    e = jnp.exp2(s + bias[b, g * 8 + hh]).astype(BF16) * allowed
                    prob[:, h * TOK : (h + 1) * TOK] = e
                o = dot(prob[...], vone[...])
                ctx[:, v0 : v0 + 128] = (o[:, 0:128] / o[:, 128:256]).astype(BF16)

        att = dot(ctx[...], wproj[b]) + bproj[pl.ds(b, 1), :]
        mid = x.astype(F32) + layer_norm(att, gain[b, 0:1, :], shift[b, 0:1, :])
        midb = mid.astype(BF16)
        for f in range(FF // 512):
            lanes = slice(f * 512, (f + 1) * 512)
            hid[:, lanes] = gelu(dot(midb, wup[b, :, lanes]) + bup[pl.ds(b, 1), lanes]).astype(BF16)
        red = dot(hid[...], wdown[b]) + bdown[pl.ds(b, 1), :]
        y = midb.astype(F32) + layer_norm(red, gain[b, 1:2, :], shift[b, 1:2, :])
        keep = jnp.logical_or(mask[i, j] == 1, b == 1)
        y = jnp.where(keep, y, x.astype(F32)).astype(BF16)
        buf[b + 1, cb, half_rows, :] = y[0 : TOK // 2]
        buf[b + 1, cb + 1, half_rows, :] = y[TOK // 2 :]

        if remote:
            @pl.when(w == ww)
            def _():
                for c in halo:
                    c.start()

            for n_ in range(nwin):
                if back[n_]:
                    @pl.when(w == 2 * nwin - 1 - n_)
                    def _(n_=n_):
                        for c in back[n_]:
                            c.start()
        return carry

    lax.fori_loop(0, 2 * nwin, window, 0)
    if remote:
        for c in halo:
            c.wait_send()
        for cs in back:
            for c in cs:
                c.wait()
    for j in range(ww):
        parts = [
            buf[2, 2 * j + b, 0:own, :].astype(F32).reshape(tile_rows, HALF, DIM) for b in range(2)
        ]
        out[:, j * WIN : (j + 1) * WIN, :] = jnp.concatenate(parts, axis=1).astype(BF16)


def body(remote, *args):
    tokens = args[0]
    tile_rows, tile_cols = tokens.shape[0], tokens.shape[1]
    ww = tile_cols // WIN
    vmem = pl.BlockSpec(memory_space=pltpu.VMEM)
    smem = pl.BlockSpec(memory_space=pltpu.SMEM)
    anym = pl.BlockSpec(memory_space=pl.ANY)
    return pl.pallas_call(
        functools.partial(kernel, remote),
        out_shape=jax.ShapeDtypeStruct(tokens.shape, BF16),
        in_specs=[anym, smem, anym, vmem, anym, vmem, anym, vmem, anym, vmem, vmem, vmem, smem, vmem],
        out_specs=vmem,
        scratch_shapes=[
            pltpu.VMEM(tokens.shape, BF16),
            pltpu.VMEM((2, DIM, 3 * DIM), BF16),
            pltpu.VMEM((2, DIM, DIM), BF16),
            pltpu.VMEM((2, DIM, FF), BF16),
            pltpu.VMEM((2, FF, DIM), BF16),
            pltpu.VMEM((3, 2 * ww + 1, (tile_rows + HALF) * HALF, DIM), BF16),
            pltpu.VMEM((2, HEADS, TOK, TOK), F32),
            pltpu.VMEM((2 * HEADS, LANES_POS), F32),
            pltpu.VMEM((2, 3 * 256, 128), F32),
            pltpu.VMEM((TOK, 4 * TOK), BF16),
            pltpu.VMEM((4 * TOK, 256), BF16),
            pltpu.VMEM((TOK, DIM), BF16),
            pltpu.VMEM((TOK, FF), BF16),
            pltpu.VMEM((256, 256), BF16),
            pltpu.SemaphoreType.DMA((5,)),
            pltpu.SemaphoreType.DMA((9,)),
            pltpu.SemaphoreType.DMA((9,)),
        ],
        compiler_params=pltpu.CompilerParams(
            collective_id=0 if remote else None,
            has_side_effects=remote,
            vmem_limit_bytes=56 * 1024 * 1024,
        ),
    )(*args)


def solution(mesh):
    return jax.shard_map(
        functools.partial(body, True),
        mesh=mesh,
        in_specs=(P("row", "col", None), P("row", "col")) + (P(),) * 12,
        out_specs=P("row", "col", None),
        check_vma=False,
    )
```

```python
import functools

import jax
import jax.numpy as jnp
from jax import lax
from jax.experimental import pallas as pl
from jax.experimental.pallas import tpu as pltpu
from jax.sharding import PartitionSpec as P

DIM = 512
HEADS = 16
HEAD_DIM = 32
FF = 2048
WIN = 16
HALF = 8
SPAN = 31
POS = 961
TOK = WIN * WIN
NORM_EPS = 1e-05
LOG2E = 1.4426950408889634
LANES_POS = 1024
CHUNK = 256
ORDER = ((0, 1, 3, 2, 4, 5), (0, 3, 4, 5, 2, 1))
HALO_AFTER = 2
FIRST = [("start", 0)] + [(p, g) for g in range(2) for p in ("q", "k", "v", "unit")] + [("head", h) for h in range(16)]
LAST = [("merge", 0), ("norm", 0)] + [("widen", f) for f in range(8)] + [("narrow", 0), ("narrow", 1), ("finish", 0)]
OPENING = (
    ("start", 0), ("q", 0), ("k", 0), ("merge", 0), ("v", 0), ("unit", 0), ("norm", 0),
    ("q", 1), ("k", 1), ("v", 1),
)
AFTER = {
    0: [("widen", 0)], 1: [("unit", 1), ("widen", 1), ("widen", 2)], 2: [("widen", 3)], 3: [("widen", 4)],
    4: [("widen", 5), ("widen", 6)], 5: [("widen", 7), ("narrow", 0)], 6: [("narrow", 1)], 7: [("finish", 0)],
}


def mixed():
    steps = list(OPENING)
    for h in range(HEADS):
        steps += [("head", h)] + AFTER.get(h, [])
    return steps


MIXED = mixed()

GELU_POLY = (
    0.7978275766755302,
    0.036469930643555554,
    -0.00012547612359992849,
    -3.0467214006275725e-05,
    1.1126326266502673e-06,
)
PENALTY = -30000.0

F32 = jnp.float32
BF16 = jnp.bfloat16
MESH = pl.DeviceIdType.MESH


def dot(a, b):
    return jnp.dot(a, b, preferred_element_type=F32)


def twice_gelu(x):
    u = x * x
    p = GELU_POLY[-1]
    for c in GELU_POLY[-2::-1]:
        p = p * u + c
    return x * (jnp.tanh(x * p) + 1.0)


def layer_norm(v, g, s):
    m = jnp.mean(v, axis=-1, keepdims=True)
    c = v - m
    var = jnp.mean(c * c, axis=-1, keepdims=True)
    return c * lax.rsqrt(var + NORM_EPS) * g + s


def spread_table(table, tscr, wscr):
    tscr[...] = jnp.zeros_like(tscr)
    for b in range(2):
        tscr[b * HEADS : (b + 1) * HEADS, 0:POS] = table[b] * LOG2E
    t = tscr[...]
    r = jnp.concatenate([pltpu.roll(t, LANES_POS - c, 1) if c else t for c in range(8)], axis=0)
    hi = r.astype(BF16)
    lo = (r - hi.astype(F32)).astype(BF16)
    rows = lax.broadcasted_iota(jnp.int32, (LANES_POS, 256), 0)
    lane = lax.broadcasted_iota(jnp.int32, (1, 256), 1)
    target = (30 - (lane >> 3)) * SPAN + 7 - (lane & 7)
    for d in range(3):
        pick = jnp.where(rows == target + 8 * d, 1.0, 0.0).astype(BF16)
        w = dot(hi, pick) + dot(lo, pick)
        for half in range(2):
            wscr[half, d * 256 : (d + 1) * 256, :] = w[:, half * 128 : (half + 1) * 128]


def expand_bias(wscr, bias, b, h):
    lane = lax.broadcasted_iota(jnp.int32, (HALF, 128), 1)
    for d in range(3):
        rows8 = pl.ds(d * 256 + b * HEADS + h, 8, stride=32)
        w0, w1 = wscr[0, rows8, :], wscr[1, rows8, :]
        for rp in range(WIN):
            o = (15 - rp) * 8
            piece = pltpu.roll(jnp.where(lane < o, w1, w0), 128 - o, 1) if o else w0
            for bp in range(2):
                bq = bp - (d - 1)
                if 0 <= bq < 2:
                    bias[b, h, bp * 128 + rp * 8 : bp * 128 + rp * 8 + 8, bq * 128 : bq * 128 + 128] = piece


def kernel(
    remote,
    tok_hbm, mask, wqkv_hbm, bqkv, wproj_hbm, bproj, wup_hbm, bup, wdown_hbm, bdown,
    gain, shift, lscale, table,
    out,
    tok, wqkv, wproj, wup, wdown, buf, bias, tscr, wscr, prob, vone, ctx, hid, same, hmask, qlab, klab, load_sem, send_sem, recv_sem,
):
    tile_rows, tile_cols = tok.shape[0], tok.shape[1]
    wh, ww = tile_rows // WIN, tile_cols // WIN
    nwin = wh * ww
    own = tile_rows * HALF
    edge_rows = HALF * HALF
    halves = 2 * ww

    loads = [[pltpu.make_async_copy(tok_hbm, tok, load_sem.at[0])], []]
    for b in range(2):
        for k, (src, dst) in enumerate(((wqkv_hbm, wqkv), (wproj_hbm, wproj), (wup_hbm, wup), (wdown_hbm, wdown))):
            loads[b].append(pltpu.make_async_copy(src.at[b], dst.at[b], load_sem.at[1 + 4 * b + k]))
    for c in loads[0]:
        c.start()

    if remote:
        row, col = lax.axis_index("row"), lax.axis_index("col")
        nrow, ncol = lax.axis_size("row"), lax.axis_size("col")
        up, down = lax.rem(row + nrow - 1, nrow), lax.rem(row + 1, nrow)
        left, right = lax.rem(col + ncol - 1, ncol), lax.rem(col + 1, ncol)
        barrier = pltpu.get_barrier_semaphore()
        for dev in ((up, col), (row, left), (up, left), (down, col), (row, right), (down, right)):
            pl.semaphore_signal(barrier, inc=1, device_id=dev, device_id_type=MESH)
        pl.semaphore_wait(barrier, 6)
        last_row = row == nrow - 1
        last_col = col == ncol - 1

        def copy(k, src, dst, dev):
            return pltpu.make_async_remote_copy(
                src_ref=src, dst_ref=dst, send_sem=send_sem.at[k], recv_sem=recv_sem.at[k],
                device_id=dev, device_id_type=MESH,
            )

        first, second = buf.at[1], buf.at[2]
        inner = pl.ds(0, edge_rows)
        outer = pl.ds(own, edge_rows)
        halo = [
            copy(0, first.at[pl.ds(0, halves), inner], first.at[pl.ds(0, halves), outer], (up, col)),
            copy(1, first.at[0, pl.ds(0, own)], first.at[halves, pl.ds(0, own)], (row, left)),
            copy(2, first.at[0, inner], first.at[halves, outer], (up, left)),
        ]
        back = [[] for _ in range(nwin)]
        k = 3
        for i in range(wh):
            for j in range(ww):
                n = i * ww + j
                low, right_edge = i == wh - 1, j == ww - 1
                start = edge_rows + i * TOK // 2
                size = TOK // 2 - (edge_rows if low else 0)
                if low:
                    cnt = 1 if right_edge else 2
                    cols = pl.ds(2 * j + 1, cnt)
                    back[n].append(copy(k, second.at[cols, outer], second.at[cols, inner], (down, col)))
                    k += 1
                if right_edge:
                    rows = pl.ds(start, size)
                    back[n].append(copy(k, second.at[halves, rows], second.at[0, rows], (row, right)))
                    k += 1
                if low and right_edge:
                    back[n].append(copy(k, second.at[halves, outer], second.at[0, inner], (down, right)))
                    k += 1
    else:
        last_row = last_col = jnp.bool_(False)

    loads[0][0].wait()
    for j in range(ww):
        t = tok[:, j * WIN : (j + 1) * WIN, :].astype(F32)
        for b in range(2):
            buf[0, 2 * j + b, 0:own, :] = t[:, b * HALF : (b + 1) * HALF, :].reshape(own, DIM).astype(BF16)

    spread_table(table, tscr, wscr)

    r256 = lax.broadcasted_iota(jnp.int32, (256, 256), 0)
    c256 = lax.broadcasted_iota(jnp.int32, (256, 256), 1)
    same[...] = jnp.where((r256 >> 5) == (c256 >> 5), 1.0, 0.0).astype(BF16)
    head_lane = lax.broadcasted_iota(jnp.int32, (WIN, 128), 1) >> 5
    for h in range(4):
        hmask[h] = jnp.where(head_lane == h, 1.0, 0.0).astype(BF16)
    token = lax.broadcasted_iota(jnp.int32, (TOK, 128), 0)
    lane128 = lax.broadcasted_iota(jnp.int32, (TOK, 128), 1)
    for case in range(4):
        label = ((token >> 6) & 1) * (case & 2) + (token >> 7) * (case & 1)
        qlab[case] = jnp.where(lane128 == label, 1.0, 0.0).astype(BF16)
        klab[case] = jnp.where(jnp.logical_or(lane128 == label, lane128 > 3), 0.0, PENALTY).astype(BF16)
    for h in range(4):
        vone[h * TOK : (h + 1) * TOK, 128:256] = jnp.where((lane128 >> 5) == h, 1.0, 0.0).astype(BF16)
    lane512 = lax.broadcasted_iota(jnp.int32, (1, DIM), 1)

    def place(w):
        b = w // nwin
        n = w % nwin
        idx = jnp.int32(0)
        for k in range(nwin):
            idx = idx + jnp.where(n == k, jnp.where(b == 0, ORDER[0][k], ORDER[1][k]), 0)
        i = idx // ww
        j = idx % ww
        cb = 2 * j + b
        rows = pl.ds(pl.multiple_of(i * (TOK // 2) + b * edge_rows, edge_rows), TOK // 2)
        return b, i, j, cb, rows

    def load_x(b, cb, rows):
        return jnp.concatenate([buf[b, cb, rows, :], buf[b, cb + 1, rows, :]], axis=0)

    def attention(w):
        b, i, j, cb, rows = place(w)
        st = {}

        def start():
            st["x"] = load_x(b, cb, rows)
            sc = jnp.zeros((1, DIM), F32)
            for h in range(HEADS):
                sc = jnp.where((lane512 >> 5) == h, lscale[b, h] * LOG2E, sc)
            st["sc"] = sc
            cut_row = jnp.logical_and(jnp.logical_and(last_row, b == 1), i == wh - 1)
            cut_col = jnp.logical_and(jnp.logical_and(last_col, b == 1), j == ww - 1)
            st["case"] = cut_row.astype(jnp.int32) * 2 + cut_col.astype(jnp.int32)

        def project(part, g):
            lanes = slice(part * DIM + g * 256, part * DIM + (g + 1) * 256)
            r = dot(st["x"], wqkv[b, :, lanes]) + bqkv[pl.ds(b, 1), lanes]
            st[part, g] = r.astype(BF16) if part == 2 else r

        def unit(g):
            lanes = slice(g * 256, (g + 1) * 256)
            qg, kg = st[0, g], st[1, g]
            q2 = dot((qg * qg).astype(BF16), same[...])
            k2 = dot((kg * kg).astype(BF16), same[...])
            st["qn", g] = (qg * (lax.rsqrt(jnp.maximum(q2, 1.0)) * st["sc"][:, lanes])).astype(BF16)
            st["kn", g] = (kg * lax.rsqrt(jnp.maximum(k2, 1.0))).astype(BF16)

        def head(h):
            h4, g = h % 4, h // 8
            here = slice((h - h4) % 8 * HEAD_DIM, (h - h4) % 8 * HEAD_DIM + 128)
            only = hmask[h4][None]
            vg = st[2, g][:, here].reshape(WIN, WIN, 128)
            vone[h4 * TOK : (h4 + 1) * TOK, 0:128] = (vg * only).reshape(TOK, 128)
            qm = (st["qn", g][:, here].reshape(WIN, WIN, 128) * only).reshape(TOK, 128)
            s = lax.dot_general(
                jnp.concatenate([qm, qlab[st["case"]]], axis=1),
                jnp.concatenate([st["kn", g][:, here], klab[st["case"]]], axis=1),
                (((1,), (1,)), ((), ())), preferred_element_type=F32,
            )
            prob[:, h4 * TOK : (h4 + 1) * TOK] = jnp.exp2(s + bias[b, h]).astype(BF16)
            if h4 == 3:
                o = dot(prob[...], vone[...])
                v0 = (h - 3) * HEAD_DIM
                ctx[:, v0 : v0 + 128] = (o[:, 0:128] * pl.reciprocal(o[:, 128:256], approx=True)).astype(BF16)

        steps = {("start", 0): start}
        for g in range(2):
            steps["unit", g] = functools.partial(unit, g)
            for part in range(3):
                steps["qkv"[part], g] = functools.partial(project, part, g)
        for h in range(HEADS):
            steps["head", h] = functools.partial(head, h)
        return steps

    def feed(w):
        b, i, j, cb, rows = place(w)
        st = {}

        def merge():
            st["x"] = load_x(b, cb, rows).astype(F32)
            st["att"] = dot(ctx[...], wproj[b]) + bproj[pl.ds(b, 1), :]

        def norm():
            mid = st["x"] + layer_norm(st["att"], gain[b, 0:1, :], shift[b, 0:1, :])
            st["mid"] = mid.astype(BF16)

        def widen(f):
            lanes = slice(f * CHUNK, (f + 1) * CHUNK)
            up_ = dot(st["mid"], wup[b, :, lanes]) + bup[pl.ds(b, 1), lanes]
            hid[:, lanes] = twice_gelu(up_).astype(BF16)

        def narrow(n):
            lanes = slice(n * 256, (n + 1) * 256)
            st["red", n] = 0.5 * dot(hid[...], wdown[b, :, lanes]) + bdown[pl.ds(b, 1), lanes]

        def finish():
            y = st["mid"].astype(F32) + layer_norm(jnp.concatenate([st["red", 0], st["red", 1]], axis=1), gain[b, 1:2, :], shift[b, 1:2, :])
            keep = jnp.logical_or(mask[i, j] == 1, b == 1)
            y = jnp.where(keep, y, st["x"]).astype(BF16)
            buf[b + 1, cb, rows, :] = y[0 : TOK // 2]
            buf[b + 1, cb + 1, rows, :] = y[TOK // 2 :]

        steps = {("merge", 0): merge, ("norm", 0): norm, ("finish", 0): finish}
        for f in range(FF // CHUNK):
            steps["widen", f] = functools.partial(widen, f)
        for n in range(2):
            steps["narrow", n] = functools.partial(narrow, n)
        return steps

    for c in loads[0][1:]:
        c.wait()
    for c in loads[1]:
        c.start()
    first_steps = attention(jnp.int32(0))
    for step in FIRST:
        if step[0] == "head":
            for b in range(2):
                expand_bias(wscr, bias, b, step[1])
        first_steps[step]()

    def both(t, carry):
        @pl.when(t == nwin)
        def _():
            for c in loads[1]:
                c.wait()

        if remote:
            @pl.when(t == nwin + 1)
            def _():
                for c in halo:
                    c.wait_recv()

        steps = {**attention(t), **feed(t - 1)}
        for step in MIXED:
            steps[step]()

        if remote:
            for pos in range(nwin):
                if ORDER[0][pos] == HALO_AFTER:
                    @pl.when(t == pos + 1)
                    def _():
                        for c in halo:
                            c.start()
                n_ = ORDER[1][pos]
                if back[n_] and pos < nwin - 1:
                    @pl.when(t == nwin + pos + 1)
                    def _(n_=n_):
                        for c in back[n_]:
                            c.start()
        return carry

    lax.fori_loop(1, 2 * nwin, both, 0)
    last_steps = feed(jnp.int32(2 * nwin - 1))
    for step in LAST:
        last_steps[step]()
    if remote:
        for c in halo:
            c.wait_send()
        for cs in back:
            for c in cs:
                c.wait()
    for j in range(ww):
        parts = [
            buf[2, 2 * j + b, 0:own, :].astype(F32).reshape(tile_rows, HALF, DIM) for b in range(2)
        ]
        out[:, j * WIN : (j + 1) * WIN, :] = jnp.concatenate(parts, axis=1).astype(BF16)


def body(remote, *args):
    tokens = args[0]
    tile_rows, tile_cols = tokens.shape[0], tokens.shape[1]
    ww = tile_cols // WIN
    vmem = pl.BlockSpec(memory_space=pltpu.VMEM)
    smem = pl.BlockSpec(memory_space=pltpu.SMEM)
    anym = pl.BlockSpec(memory_space=pl.ANY)
    return pl.pallas_call(
        functools.partial(kernel, remote),
        out_shape=jax.ShapeDtypeStruct(tokens.shape, BF16),
        in_specs=[anym, smem, anym, vmem, anym, vmem, anym, vmem, anym, vmem, vmem, vmem, smem, vmem],
        out_specs=vmem,
        scratch_shapes=[
            pltpu.VMEM(tokens.shape, BF16),
            pltpu.VMEM((2, DIM, 3 * DIM), BF16),
            pltpu.VMEM((2, DIM, DIM), BF16),
            pltpu.VMEM((2, DIM, FF), BF16),
            pltpu.VMEM((2, FF, DIM), BF16),
            pltpu.VMEM((3, 2 * ww + 1, (tile_rows + HALF) * HALF, DIM), BF16),
            pltpu.VMEM((2, HEADS, TOK, TOK), F32),
            pltpu.VMEM((2 * HEADS, LANES_POS), F32),
            pltpu.VMEM((2, 3 * 256, 128), F32),
            pltpu.VMEM((TOK, 4 * TOK), BF16),
            pltpu.VMEM((4 * TOK, 256), BF16),
            pltpu.VMEM((TOK, DIM), BF16),
            pltpu.VMEM((TOK, FF), BF16),
            pltpu.VMEM((256, 256), BF16),
            pltpu.VMEM((4, WIN, 128), BF16),
            pltpu.VMEM((4, TOK, 128), BF16),
            pltpu.VMEM((4, TOK, 128), BF16),
            pltpu.SemaphoreType.DMA((9,)),
            pltpu.SemaphoreType.DMA((9,)),
            pltpu.SemaphoreType.DMA((9,)),
        ],
        compiler_params=pltpu.CompilerParams(
            collective_id=0 if remote else None,
            has_side_effects=remote,
            vmem_limit_bytes=56 * 1024 * 1024,
        ),
    )(*args)


def solution(mesh):
    return jax.shard_map(
        functools.partial(body, True),
        mesh=mesh,
        in_specs=(P("row", "col", None), P("row", "col")) + (P(),) * 12,
        out_specs=P("row", "col", None),
        check_vma=False,
    )
```

```python
import functools

import jax
import jax.numpy as jnp
from jax import lax
from jax.experimental import pallas as pl
from jax.experimental.pallas import tpu as pltpu
from jax.sharding import PartitionSpec as P

DIM = 512
HEADS = 16
HEAD_DIM = 32
FF = 2048
WIN = 16
HALF = 8
SPAN = 31
POS = 961
TOK = WIN * WIN
NORM_EPS = 1e-05
LOG2E = 1.4426950408889634
LANES_POS = 1024
CHUNK = 256
ORDER = ((0, 1, 3, 4, 2, 5), (0, 3, 2, 4, 5, 1))
PROJECT = [("start", 0)] + [(p, g) for g in range(2) for p in ("q", "k", "v", "unit")]
LAST = (
    [("merge", 0)] + [("norm", c) for c in range(4)] + [("widen", f) for f in range(8)]
    + [("narrow", 0), ("narrow", 1)] + [("finish", c) for c in range(4)]
)
AFTER = {
    0: [("merge", 0)],
    1: [("norm", 0), ("q", 0)],
    2: [("norm", 1), ("k", 0)],
    3: [("norm", 2), ("v", 0), ("unit", 0)],
    4: [("norm", 3), ("q", 1)],
    5: [("widen", 0), ("k", 1)],
    6: [("widen", 1), ("v", 1), ("unit", 1)],
    7: [("widen", 2)],
    8: [("widen", 3), ("widen", 4)],
    9: [("widen", 5)],
    10: [("widen", 6)],
    11: [("widen", 7), ("narrow", 0)],
    12: [("narrow", 1)],
    13: [("finish", 0)],
    14: [("finish", 1), ("finish", 2)],
    15: [("finish", 3)],
}

GELU_POLY = (
    0.7978275766755302,
    0.036469930643555554,
    -0.00012547612359992849,
    -3.0467214006275725e-05,
    1.1126326266502673e-06,
)
PENALTY = -30000.0
ROWS = 64

F32 = jnp.float32
BF16 = jnp.bfloat16
MESH = pl.DeviceIdType.MESH


def dot(a, b):
    return jnp.dot(a, b, preferred_element_type=F32)


def twice_gelu(x):
    v = x.astype(BF16)
    u = v * v
    p = jnp.asarray(GELU_POLY[-1], BF16)
    for c in GELU_POLY[-2::-1]:
        p = p * u + jnp.asarray(c, BF16)
    return x * (jnp.tanh(v * p).astype(F32) + 1.0)


def layer_norm(v, g, s, eps):
    m = jnp.mean(v, axis=-1, keepdims=True)
    c = v - m
    var = jnp.mean(c * c, axis=-1, keepdims=True)
    return c * lax.rsqrt(var + eps) * g + s


def spread_table(table, tscr, wscr):
    tscr[...] = jnp.zeros_like(tscr)
    for b in range(2):
        tscr[b * HEADS : (b + 1) * HEADS, 0:POS] = jnp.exp2(table[b] * LOG2E)
    t = tscr[...]
    r = jnp.concatenate([pltpu.roll(t, LANES_POS - c, 1) if c else t for c in range(8)], axis=0).astype(BF16)
    rows = lax.broadcasted_iota(jnp.int32, (LANES_POS, 256), 0)
    lane = lax.broadcasted_iota(jnp.int32, (1, 256), 1)
    target = (30 - (lane >> 3)) * SPAN + 7 - (lane & 7)
    for d in range(3):
        pick = jnp.where(rows == target + 8 * d, 1.0, 0.0).astype(BF16)
        w = dot(r, pick)
        for half in range(2):
            wscr[half, d * 256 : (d + 1) * 256, :] = w[:, half * 128 : (half + 1) * 128]


def expand_bias(wscr, bias, b, h):
    lane = lax.broadcasted_iota(jnp.int32, (HALF, 128), 1)
    for d in range(3):
        rows8 = pl.ds(d * 256 + b * HEADS + h, 8, stride=32)
        w0, w1 = wscr[0, rows8, :], wscr[1, rows8, :]
        for rp in range(0, WIN, 2):
            pair = []
            for o in ((15 - rp) * 8, (14 - rp) * 8):
                pair.append(pltpu.roll(jnp.where(lane < o, w1, w0), 128 - o, 1) if o else w0)
            piece = jnp.concatenate(pair, axis=0).astype(BF16)
            for bp in range(2):
                bq = bp - (d - 1)
                if 0 <= bq < 2:
                    bias[b, h, bp * 128 + rp * 8 : bp * 128 + rp * 8 + 16, bq * 128 : bq * 128 + 128] = piece


def kernel(
    remote,
    tok_hbm, mask, wqkv_hbm, bqkv, wproj_hbm, bproj, wup_hbm, bup, wdown_hbm, bdown,
    gain, shift, lscale, table,
    out,
    tok, wqkv, wproj, wup, wdown, buf, bias, tscr, wscr, prob, vone, ctx, hid, same, hmask, unit_qkv, qlab, klab, load_sem, send_sem, recv_sem,
):
    tile_rows, tile_cols = tok.shape[0], tok.shape[1]
    wh, ww = tile_rows // WIN, tile_cols // WIN
    nwin = wh * ww
    own = tile_rows * HALF
    edge_rows = HALF * HALF
    halves = 2 * ww

    loads = [[pltpu.make_async_copy(tok_hbm, tok, load_sem.at[0])], []]
    for b in range(2):
        for k, (src, dst) in enumerate(((wqkv_hbm, wqkv), (wproj_hbm, wproj), (wup_hbm, wup), (wdown_hbm, wdown))):
            loads[b].append(pltpu.make_async_copy(src.at[b], dst.at[b], load_sem.at[1 + 4 * b + k]))
    for c in loads[0]:
        c.start()

    if remote:
        row, col = lax.axis_index("row"), lax.axis_index("col")
        nrow, ncol = lax.axis_size("row"), lax.axis_size("col")
        up, down = lax.rem(row + nrow - 1, nrow), lax.rem(row + 1, nrow)
        left, right = lax.rem(col + ncol - 1, ncol), lax.rem(col + 1, ncol)
        barrier = pltpu.get_barrier_semaphore()
        for dev in ((up, col), (row, left), (up, left), (down, col), (row, right), (down, right)):
            pl.semaphore_signal(barrier, inc=1, device_id=dev, device_id_type=MESH)
        last_row = row == nrow - 1
        last_col = col == ncol - 1

        def copy(k, src, dst, dev):
            return pltpu.make_async_remote_copy(
                src_ref=src, dst_ref=dst, send_sem=send_sem.at[k], recv_sem=recv_sem.at[k],
                device_id=dev, device_id_type=MESH,
            )

        stage1, stage2 = buf.at[1], buf.at[2]
        inner = pl.ds(0, edge_rows)
        outer = pl.ds(own, edge_rows)
        halo = [
            copy(0, stage1.at[pl.ds(0, halves - 2), inner], stage1.at[pl.ds(0, halves - 2), outer], (up, col)),
            copy(1, stage1.at[0, pl.ds(0, own)], stage1.at[halves, pl.ds(0, own)], (row, left)),
            copy(2, stage1.at[0, inner], stage1.at[halves, outer], (up, left)),
            copy(3, stage1.at[pl.ds(halves - 2, 2), inner], stage1.at[pl.ds(halves - 2, 2), outer], (up, col)),
        ]
        back = [[] for _ in range(nwin)]
        k = 4
        for i in range(wh):
            for j in range(ww):
                n = i * ww + j
                low, right_edge = i == wh - 1, j == ww - 1
                start = edge_rows + i * TOK // 2
                size = TOK // 2 - (edge_rows if low else 0)
                if low:
                    cnt = 1 if right_edge else 2
                    cols = pl.ds(2 * j + 1, cnt)
                    back[n].append(copy(k, stage2.at[cols, outer], stage2.at[cols, inner], (down, col)))
                    k += 1
                if right_edge:
                    rows = pl.ds(start, size)
                    back[n].append(copy(k, stage2.at[halves, rows], stage2.at[0, rows], (row, right)))
                    k += 1
                if low and right_edge:
                    back[n].append(copy(k, stage2.at[halves, outer], stage2.at[0, inner], (down, right)))
                    k += 1
    else:
        last_row = last_col = jnp.bool_(False)

    loads[0][0].wait()
    for j in range(ww):
        t = tok[:, j * WIN : (j + 1) * WIN, :].astype(F32)
        for b in range(2):
            buf[0, 2 * j + b, 0:own, :] = t[:, b * HALF : (b + 1) * HALF, :].reshape(own, DIM).astype(BF16)

    spread_table(table, tscr, wscr)

    r256 = lax.broadcasted_iota(jnp.int32, (256, 256), 0)
    c256 = lax.broadcasted_iota(jnp.int32, (256, 256), 1)
    same[...] = jnp.where((r256 >> 5) == (c256 >> 5), 1.0, 0.0).astype(BF16)
    head_lane = lax.broadcasted_iota(jnp.int32, (WIN, 128), 1) >> 5
    for h in range(4):
        hmask[h] = jnp.where(head_lane == h, 1.0, 0.0).astype(BF16)
    token = lax.broadcasted_iota(jnp.int32, (TOK, 128), 0)
    lane128 = lax.broadcasted_iota(jnp.int32, (TOK, 128), 1)
    for case in range(4):
        label = ((token >> 6) & 1) * (case & 2) + (token >> 7) * (case & 1)
        qlab[case] = jnp.where(lane128 == label, 1.0, 0.0).astype(BF16)
        klab[case] = jnp.where(jnp.logical_or(lane128 == label, lane128 > 3), 0.0, PENALTY).astype(BF16)
    for h in range(4):
        vone[h * TOK : (h + 1) * TOK, 128:256] = jnp.where((lane128 >> 5) == h, 1.0, 0.0).astype(BF16)
    lane512 = lax.broadcasted_iota(jnp.int32, (1, DIM), 1)

    def place(w):
        b = w // nwin
        n = w % nwin
        idx = jnp.int32(0)
        for k in range(nwin):
            idx = idx + jnp.where(n == k, jnp.where(b == 0, ORDER[0][k], ORDER[1][k]), 0)
        i = idx // ww
        j = idx % ww
        cb = 2 * j + b
        start = pl.multiple_of(i * (TOK // 2) + b * edge_rows, edge_rows)
        return b, i, j, cb, start

    def load_x(b, cb, start):
        rows = pl.ds(start, TOK // 2)
        return jnp.concatenate([buf[b, cb, rows, :], buf[b, cb + 1, rows, :]], axis=0)

    def attention(w):
        b, i, j, cb, start = place(w)
        st = {}

        def begin():
            st["x"] = load_x(b, cb, start)
            sc = jnp.zeros((1, DIM), F32)
            for h in range(HEADS):
                sc = jnp.where((lane512 >> 5) == h, lscale[b, h] * LOG2E, sc)
            st["sc"] = sc

        def fetch():
            cut_row = jnp.logical_and(jnp.logical_and(last_row, b == 1), i == wh - 1)
            cut_col = jnp.logical_and(jnp.logical_and(last_col, b == 1), j == ww - 1)
            st["case"] = cut_row.astype(jnp.int32) * 2 + cut_col.astype(jnp.int32)
            for g in range(2):
                for n, name in enumerate(("qn", "kn", "vn")):
                    st[name, g] = unit_qkv[n, g]

        def project(part, g):
            lanes = slice(part * DIM + g * 256, part * DIM + (g + 1) * 256)
            r = dot(st["x"], wqkv[b, :, lanes]) + bqkv[pl.ds(b, 1), lanes]
            if part == 2:
                unit_qkv[2, g] = r.astype(BF16)
            else:
                st[part, g] = r

        def unit(g):
            lanes = slice(g * 256, (g + 1) * 256)
            qg, kg = st[0, g], st[1, g]
            q2 = dot((qg * qg).astype(BF16), same[...])
            k2 = dot((kg * kg).astype(BF16), same[...])
            unit_qkv[0, g] = (qg * (lax.rsqrt(jnp.maximum(q2, 1.0)) * st["sc"][:, lanes])).astype(BF16)
            unit_qkv[1, g] = (kg * lax.rsqrt(jnp.maximum(k2, 1.0))).astype(BF16)

        def head(h):
            h4, g = h % 4, h // 8
            here = slice((h - h4) % 8 * HEAD_DIM, (h - h4) % 8 * HEAD_DIM + 128)
            only = hmask[h4][None]
            vg = st["vn", g][:, here].reshape(WIN, WIN, 128)
            vone[h4 * TOK : (h4 + 1) * TOK, 0:128] = (vg * only).reshape(TOK, 128)
            qm = (st["qn", g][:, here].reshape(WIN, WIN, 128) * only).reshape(TOK, 128)
            s = lax.dot_general(
                jnp.concatenate([qm, qlab[st["case"]]], axis=1),
                jnp.concatenate([st["kn", g][:, here], klab[st["case"]]], axis=1),
                (((1,), (1,)), ((), ())), preferred_element_type=F32,
            )
            prob[:, h4 * TOK : (h4 + 1) * TOK] = jnp.exp2(s).astype(BF16) * bias[b, h]
            if h4 == 3:
                o = dot(prob[...], vone[...])
                v0 = (h - 3) * HEAD_DIM
                ctx[:, v0 : v0 + 128] = (o[:, 0:128] * pl.reciprocal(o[:, 128:256], approx=True)).astype(BF16)

        steps = {("start", 0): begin, ("fetch", 0): fetch}
        for g in range(2):
            steps["unit", g] = functools.partial(unit, g)
            for part in range(3):
                steps["qkv"[part], g] = functools.partial(project, part, g)
        for h in range(HEADS):
            steps["head", h] = functools.partial(head, h)
        return steps

    def feed(w):
        b, i, j, cb, start = place(w)
        st = {}

        def merge():
            st["x"] = load_x(b, cb, start).astype(F32)
            st["att"] = dot(ctx[...], wproj[b]) + bproj[pl.ds(b, 1), :]

        def norm(c):
            part = slice(c * ROWS, (c + 1) * ROWS)
            mid = st["x"][part] + layer_norm(st["att"][part], gain[b, 0:1, :], shift[b, 0:1, :], NORM_EPS)
            st["mid", c] = mid.astype(BF16)
            if c == TOK // ROWS - 1:
                st["mid"] = jnp.concatenate([st["mid", k] for k in range(TOK // ROWS)], axis=0)

        def widen(f):
            lanes = slice(f * CHUNK, (f + 1) * CHUNK)
            up_ = dot(st["mid"], wup[b, :, lanes]) + bup[pl.ds(b, 1), lanes]
            hid[:, lanes] = twice_gelu(up_).astype(BF16)

        def narrow(n):
            lanes = slice(n * 256, (n + 1) * 256)
            st["red", n] = dot(hid[...], wdown[b, :, lanes]) + 2.0 * bdown[pl.ds(b, 1), lanes]

        def finish(c):
            part = slice(c * ROWS, (c + 1) * ROWS)
            red = jnp.concatenate([st["red", 0][part], st["red", 1][part]], axis=1)
            y = st["mid", c].astype(F32) + layer_norm(red, gain[b, 1:2, :], shift[b, 1:2, :], 4.0 * NORM_EPS)
            keep = jnp.logical_or(mask[i, j] == 1, b == 1)
            y = jnp.where(keep, y, st["x"][part]).astype(BF16)
            per = TOK // 2 // ROWS
            buf[b + 1, cb + c // per, pl.ds(pl.multiple_of(start + c % per * ROWS, ROWS), ROWS), :] = y

        steps = {("merge", 0): merge}
        for c in range(TOK // ROWS):
            steps["norm", c] = functools.partial(norm, c)
            steps["finish", c] = functools.partial(finish, c)
        for f in range(FF // CHUNK):
            steps["widen", f] = functools.partial(widen, f)
        for n in range(2):
            steps["narrow", n] = functools.partial(narrow, n)
        return steps

    for c in loads[0][1:]:
        c.wait()
    for c in loads[1]:
        c.start()
    first, ahead = attention(jnp.int32(0)), attention(jnp.int32(1))
    for step in PROJECT:
        first[step]()
    first["fetch", 0]()
    for h in range(HEADS):
        for b in range(2):
            expand_bias(wscr, bias, b, h)
        first["head", h]()
    for step in PROJECT:
        ahead[step]()

    def both(t, carry):
        @pl.when(t == nwin - 1)
        def _():
            for c in loads[1]:
                c.wait()

        if remote:
            @pl.when(t == nwin)
            def _():
                halo[0].wait_recv()

            @pl.when(t == nwin + 1)
            def _():
                halo[1].wait_recv()

            @pl.when(t == nwin + 2)
            def _():
                halo[2].wait_recv()
                halo[3].wait_recv()

        now, ahead, behind = attention(t), attention(jnp.minimum(t + 1, 2 * nwin - 1)), feed(t - 1)
        now["fetch", 0]()
        ahead["start", 0]()
        for h in range(HEADS):
            now["head", h]()
            for step in AFTER.get(h, ()):
                (behind if step in behind else ahead)[step]()

        if remote:
            @pl.when(t == 2)
            def _():
                pl.semaphore_wait(barrier, 6)
                halo[0].start()

            @pl.when(t == 3)
            def _():
                halo[1].start()
                halo[2].start()

            @pl.when(t == 5)
            def _():
                halo[3].start()

            for pos in range(nwin):
                n_ = ORDER[1][pos]
                if back[n_] and pos < nwin - 1:
                    @pl.when(t == nwin + pos + 1)
                    def _(n_=n_):
                        for c in back[n_]:
                            c.start()
        return carry

    lax.fori_loop(1, 2 * nwin, both, 0)
    last_steps = feed(jnp.int32(2 * nwin - 1))
    for step in LAST:
        last_steps[step]()
    if remote:
        for c in halo:
            c.wait_send()
        for cs in back:
            for c in cs:
                c.wait()
    for j in range(ww):
        parts = [
            buf[2, 2 * j + b, 0:own, :].astype(F32).reshape(tile_rows, HALF, DIM) for b in range(2)
        ]
        out[:, j * WIN : (j + 1) * WIN, :] = jnp.concatenate(parts, axis=1).astype(BF16)


def body(remote, *args):
    tokens = args[0]
    tile_rows, tile_cols = tokens.shape[0], tokens.shape[1]
    ww = tile_cols // WIN
    vmem = pl.BlockSpec(memory_space=pltpu.VMEM)
    smem = pl.BlockSpec(memory_space=pltpu.SMEM)
    anym = pl.BlockSpec(memory_space=pl.ANY)
    return pl.pallas_call(
        functools.partial(kernel, remote),
        out_shape=jax.ShapeDtypeStruct(tokens.shape, BF16),
        in_specs=[anym, smem, anym, vmem, anym, vmem, anym, vmem, anym, vmem, vmem, vmem, smem, vmem],
        out_specs=vmem,
        scratch_shapes=[
            pltpu.VMEM(tokens.shape, BF16),
            pltpu.VMEM((2, DIM, 3 * DIM), BF16),
            pltpu.VMEM((2, DIM, DIM), BF16),
            pltpu.VMEM((2, DIM, FF), BF16),
            pltpu.VMEM((2, FF, DIM), BF16),
            pltpu.VMEM((3, 2 * ww + 1, (tile_rows + HALF) * HALF, DIM), BF16),
            pltpu.VMEM((2, HEADS, TOK, TOK), BF16),
            pltpu.VMEM((2 * HEADS, LANES_POS), F32),
            pltpu.VMEM((2, 3 * 256, 128), F32),
            pltpu.VMEM((TOK, 4 * TOK), BF16),
            pltpu.VMEM((4 * TOK, 256), BF16),
            pltpu.VMEM((TOK, DIM), BF16),
            pltpu.VMEM((TOK, FF), BF16),
            pltpu.VMEM((256, 256), BF16),
            pltpu.VMEM((4, WIN, 128), BF16),
            pltpu.VMEM((3, 2, TOK, 256), BF16),
            pltpu.VMEM((4, TOK, 128), BF16),
            pltpu.VMEM((4, TOK, 128), BF16),
            pltpu.SemaphoreType.DMA((9,)),
            pltpu.SemaphoreType.DMA((10,)),
            pltpu.SemaphoreType.DMA((10,)),
        ],
        compiler_params=pltpu.CompilerParams(
            collective_id=0 if remote else None,
            has_side_effects=remote,
            vmem_limit_bytes=56 * 1024 * 1024,
        ),
    )(*args)


def solution(mesh):
    return jax.shard_map(
        functools.partial(body, True),
        mesh=mesh,
        in_specs=(P("row", "col", None), P("row", "col")) + (P(),) * 12,
        out_specs=P("row", "col", None),
        check_vma=False,
    )
```

```python
import functools

import jax
import jax.numpy as jnp
from jax import lax
from jax.experimental import pallas as pl
from jax.experimental.pallas import tpu as pltpu
from jax.sharding import PartitionSpec as P

DIM = 512
HEADS = 16
HEAD_DIM = 32
FF = 2048
WIN = 16
HALF = 8
SPAN = 31
POS = 961
TOK = WIN * WIN
NORM_EPS = 1e-05
LOG2E = 1.4426950408889634
LANES_POS = 1024
CHUNK = 256
ORDER = ((0, 1, 3, 4, 2, 5), (0, 3, 2, 4, 5, 1))
PROJECT = [("start", 0)] + [(p, g) for g in range(2) for p in ("q", "k", "v", "unit")]
LAST = (
    [("merge", 0)] + [("norm", c) for c in range(4)] + [("widen", f) for f in range(8)]
    + [("narrow", 0), ("narrow", 1)] + [("finish", c) for c in range(4)]
)
SPREAD = {
    1: [("start", 0), ("q", 0)], 3: [("k", 0)], 5: [("v", 0)], 7: [("unit", 0)], 9: [("q", 1)], 11: [("k", 1)], 13: [("v", 1)], 14: [("unit", 1)],
}
AFTER = {
    0: [("merge", 0), ("q", 0)],
    1: [("norm", 0), ("k", 0)],
    2: [("norm", 1), ("v", 0), ("unit", 0)],
    3: [("norm", 2), ("norm", 3), ("q", 1)],
    4: [("widen", 0), ("k", 1)],
    5: [("widen", 1)],
    6: [("widen", 2)],
    7: [("widen", 3)],
    8: [("widen", 4)],
    9: [("widen", 5)],
    10: [("widen", 6)],
    11: [("widen", 7)],
    12: [("narrow", 0)],
    13: [("narrow", 1), ("finish", 0)],
    14: [("finish", 1), ("finish", 2), ("v", 1)],
    15: [("finish", 3), ("unit", 1)],
}

GELU_POLY = (
    0.7978275766755302,
    0.036469930643555554,
    -0.00012547612359992849,
    -3.0467214006275725e-05,
    1.1126326266502673e-06,
)
PENALTY = -30000.0
ROWS = 64
OUT_ROWS = 16

F32 = jnp.float32
BF16 = jnp.bfloat16
MESH = pl.DeviceIdType.MESH


def dot(a, b):
    return jnp.dot(a, b, preferred_element_type=F32)


def twice_gelu(x):
    v = x.astype(BF16)
    u = v * v
    p = jnp.asarray(GELU_POLY[-1], BF16)
    for c in GELU_POLY[-2::-1]:
        p = p * u + jnp.asarray(c, BF16)
    return v * (jnp.tanh(v * p) + jnp.asarray(1.0, BF16))


def layer_norm(v, g, s, eps):
    m = jnp.mean(v, axis=-1, keepdims=True)
    c = v - m
    var = jnp.mean(c * c, axis=-1, keepdims=True)
    return c * lax.rsqrt(var + eps) * g + s


def spread_table(table, tscr, wscr):
    tscr[...] = jnp.zeros_like(tscr)
    for b in range(2):
        tscr[b * HEADS : (b + 1) * HEADS, 0:POS] = jnp.exp2(table[b] * LOG2E)
    t = tscr[...]
    r = jnp.concatenate([pltpu.roll(t, LANES_POS - c, 1) if c else t for c in range(8)], axis=0).astype(BF16)
    rows = lax.broadcasted_iota(jnp.int32, (LANES_POS, 256), 0)
    lane = lax.broadcasted_iota(jnp.int32, (1, 256), 1)
    target = (30 - (lane >> 3)) * SPAN + 7 - (lane & 7)
    for d in range(3):
        pick = jnp.where(rows == target + 8 * d, 1.0, 0.0).astype(BF16)
        w = dot(r, pick)
        for half in range(2):
            wscr[half, d * 256 : (d + 1) * 256, :] = w[:, half * 128 : (half + 1) * 128]


def expand_bias(wscr, bias, b, h):
    lane = lax.broadcasted_iota(jnp.int32, (HALF, 128), 1)
    for d in range(3):
        rows8 = pl.ds(d * 256 + b * HEADS + h, 8, stride=32)
        w0, w1 = wscr[0, rows8, :], wscr[1, rows8, :]
        for rp in range(0, WIN, 2):
            pair = []
            for o in ((15 - rp) * 8, (14 - rp) * 8):
                pair.append(pltpu.roll(jnp.where(lane < o, w1, w0), 128 - o, 1) if o else w0)
            piece = jnp.concatenate(pair, axis=0).astype(BF16)
            for bp in range(2):
                bq = bp - (d - 1)
                if 0 <= bq < 2:
                    bias[b, h, bp * 128 + rp * 8 : bp * 128 + rp * 8 + 16, bq * 128 : bq * 128 + 128] = piece


def kernel(
    remote,
    tok_hbm, mask, wqkv_hbm, bqkv, wproj_hbm, bproj, wup_hbm, bup, wdown_hbm, bdown,
    gain, shift, lscale, table,
    out,
    tok, wqkv, wproj, wup, wdown, buf, bias, tscr, wscr, prob, vone, ctx, hid, same, hmask, unit_qkv, qlab, klab, load_sem, out_sem, send_sem, recv_sem,
):
    tile_rows, tile_cols = tok.shape[0], tok.shape[1]
    wh, ww = tile_rows // WIN, tile_cols // WIN
    nwin = wh * ww
    own = tile_rows * HALF
    edge_rows = HALF * HALF
    halves = 2 * ww

    loads = [[pltpu.make_async_copy(tok_hbm, tok, load_sem.at[0])], []]
    for b in range(2):
        for k, (src, dst) in enumerate(((wqkv_hbm, wqkv), (wproj_hbm, wproj), (wup_hbm, wup), (wdown_hbm, wdown))):
            loads[b].append(pltpu.make_async_copy(src.at[b], dst.at[b], load_sem.at[1 + 4 * b + k]))
    for c in loads[0]:
        c.start()

    if remote:
        row, col = lax.axis_index("row"), lax.axis_index("col")
        nrow, ncol = lax.axis_size("row"), lax.axis_size("col")
        up, down = lax.rem(row + nrow - 1, nrow), lax.rem(row + 1, nrow)
        left, right = lax.rem(col + ncol - 1, ncol), lax.rem(col + 1, ncol)
        barrier = pltpu.get_barrier_semaphore()
        for dev in ((up, col), (row, left), (up, left), (down, col), (row, right), (down, right)):
            pl.semaphore_signal(barrier, inc=1, device_id=dev, device_id_type=MESH)
        last_row = row == nrow - 1
        last_col = col == ncol - 1

        def copy(k, src, dst, dev):
            return pltpu.make_async_remote_copy(
                src_ref=src, dst_ref=dst, send_sem=send_sem.at[k], recv_sem=recv_sem.at[k],
                device_id=dev, device_id_type=MESH,
            )

        stage1, stage2 = buf.at[1], buf.at[2]
        inner = pl.ds(0, edge_rows)
        outer = pl.ds(own, edge_rows)
        halo = [
            copy(0, stage1.at[pl.ds(0, halves - 2), inner], stage1.at[pl.ds(0, halves - 2), outer], (up, col)),
            copy(1, stage1.at[0, pl.ds(0, own)], stage1.at[halves, pl.ds(0, own)], (row, left)),
            copy(2, stage1.at[0, inner], stage1.at[halves, outer], (up, left)),
            copy(3, stage1.at[pl.ds(halves - 2, 2), inner], stage1.at[pl.ds(halves - 2, 2), outer], (up, col)),
        ]
        back = [[] for _ in range(nwin)]
        k = 4
        for i in range(wh):
            for j in range(ww):
                n = i * ww + j
                low, right_edge = i == wh - 1, j == ww - 1
                start = edge_rows + i * TOK // 2
                size = TOK // 2 - (edge_rows if low else 0)
                if low:
                    cnt = 1 if right_edge else 2
                    cols = pl.ds(2 * j + 1, cnt)
                    back[n].append(copy(k, stage2.at[cols, outer], stage2.at[cols, inner], (down, col)))
                    k += 1
                if right_edge:
                    rows = pl.ds(start, size)
                    back[n].append(copy(k, stage2.at[halves, rows], stage2.at[0, rows], (row, right)))
                    k += 1
                if low and right_edge:
                    back[n].append(copy(k, stage2.at[halves, outer], stage2.at[0, inner], (down, right)))
                    k += 1
    else:
        last_row = last_col = jnp.bool_(False)

    loads[0][0].wait()
    for j in range(ww):
        t = tok[:, j * WIN : (j + 1) * WIN, :].astype(F32)
        for b in range(2):
            buf[0, 2 * j + b, 0:own, :] = t[:, b * HALF : (b + 1) * HALF, :].reshape(own, DIM).astype(BF16)

    spread_table(table, tscr, wscr)

    r256 = lax.broadcasted_iota(jnp.int32, (256, 256), 0)
    c256 = lax.broadcasted_iota(jnp.int32, (256, 256), 1)
    same[...] = jnp.where((r256 >> 5) == (c256 >> 5), 1.0, 0.0).astype(BF16)
    head_lane = lax.broadcasted_iota(jnp.int32, (WIN, 128), 1) >> 5
    for h in range(4):
        hmask[h] = jnp.where(head_lane == h, 1.0, 0.0).astype(BF16)
    token = lax.broadcasted_iota(jnp.int32, (TOK, 128), 0)
    lane128 = lax.broadcasted_iota(jnp.int32, (TOK, 128), 1)
    for case in range(4):
        label = ((token >> 6) & 1) * (case & 2) + (token >> 7) * (case & 1)
        qlab[case] = jnp.where(lane128 == label, 1.0, 0.0).astype(BF16)
        klab[case] = jnp.where(jnp.logical_or(lane128 == label, lane128 > 3), 0.0, PENALTY).astype(BF16)
    for h in range(4):
        vone[h * TOK : (h + 1) * TOK, 128:256] = jnp.where((lane128 >> 5) == h, 1.0, 0.0).astype(BF16)
    lane512 = lax.broadcasted_iota(jnp.int32, (1, DIM), 1)

    def place(w):
        b = w // nwin
        n = w % nwin
        idx = jnp.int32(0)
        for k in range(nwin):
            idx = idx + jnp.where(n == k, jnp.where(b == 0, ORDER[0][k], ORDER[1][k]), 0)
        i = idx // ww
        j = idx % ww
        cb = 2 * j + b
        start = pl.multiple_of(i * (TOK // 2) + b * edge_rows, edge_rows)
        return b, i, j, cb, start

    def load_x(b, cb, start):
        rows = pl.ds(start, TOK // 2)
        return jnp.concatenate([buf[b, cb, rows, :], buf[b, cb + 1, rows, :]], axis=0)

    def attention(w):
        b, i, j, cb, start = place(w)
        st = {}

        def begin():
            st["x"] = load_x(b, cb, start)
            sc = jnp.zeros((1, DIM), F32)
            for h in range(HEADS):
                sc = jnp.where((lane512 >> 5) == h, lscale[b, h] * LOG2E, sc)
            st["sc"] = sc

        def fetch():
            cut_row = jnp.logical_and(jnp.logical_and(last_row, b == 1), i == wh - 1)
            cut_col = jnp.logical_and(jnp.logical_and(last_col, b == 1), j == ww - 1)
            st["case"] = cut_row.astype(jnp.int32) * 2 + cut_col.astype(jnp.int32)
            for g in range(2):
                for n, name in enumerate(("qn", "kn", "vn")):
                    st[name, g] = unit_qkv[n, g]

        def project(part, g):
            lanes = slice(part * DIM + g * 256, part * DIM + (g + 1) * 256)
            r = dot(st["x"], wqkv[b, :, lanes]) + bqkv[pl.ds(b, 1), lanes]
            if part == 2:
                unit_qkv[2, g] = r.astype(BF16)
            else:
                st[part, g] = r

        def unit(g):
            lanes = slice(g * 256, (g + 1) * 256)
            qg, kg = st[0, g], st[1, g]
            q2 = dot((qg * qg).astype(BF16), same[...])
            k2 = dot((kg * kg).astype(BF16), same[...])
            unit_qkv[0, g] = (qg * (lax.rsqrt(jnp.maximum(q2, 1.0)) * st["sc"][:, lanes])).astype(BF16)
            unit_qkv[1, g] = (kg * lax.rsqrt(jnp.maximum(k2, 1.0))).astype(BF16)

        def head(h):
            h4, g = h % 4, h // 8
            here = slice((h - h4) % 8 * HEAD_DIM, (h - h4) % 8 * HEAD_DIM + 128)
            only = hmask[h4][None]
            vg = st["vn", g][:, here].reshape(WIN, WIN, 128)
            vone[h4 * TOK : (h4 + 1) * TOK, 0:128] = (vg * only).reshape(TOK, 128)
            qm = (st["qn", g][:, here].reshape(WIN, WIN, 128) * only).reshape(TOK, 128)
            s = lax.dot_general(
                jnp.concatenate([qm, qlab[st["case"]]], axis=1),
                jnp.concatenate([st["kn", g][:, here], klab[st["case"]]], axis=1),
                (((1,), (1,)), ((), ())), preferred_element_type=F32,
            )
            prob[:, h4 * TOK : (h4 + 1) * TOK] = jnp.exp2(s).astype(BF16) * bias[b, h]
            if h4 == 3:
                o = dot(prob[...], vone[...])
                v0 = (h - 3) * HEAD_DIM
                ctx[:, v0 : v0 + 128] = (o[:, 0:128] * pl.reciprocal(o[:, 128:256], approx=True)).astype(BF16)

        steps = {("start", 0): begin, ("fetch", 0): fetch}
        for g in range(2):
            steps["unit", g] = functools.partial(unit, g)
            for part in range(3):
                steps["qkv"[part], g] = functools.partial(project, part, g)
        for h in range(HEADS):
            steps["head", h] = functools.partial(head, h)
        return steps

    def feed(w):
        b, i, j, cb, start = place(w)
        st = {}

        def merge():
            st["x"] = load_x(b, cb, start).astype(F32)
            st["att"] = dot(ctx[...], wproj[b]) + bproj[pl.ds(b, 1), :]

        def norm(c):
            part = slice(c * ROWS, (c + 1) * ROWS)
            mid = st["x"][part] + layer_norm(st["att"][part], gain[b, 0:1, :], shift[b, 0:1, :], NORM_EPS)
            st["mid", c] = mid.astype(BF16)
            if c == TOK // ROWS - 1:
                st["mid"] = jnp.concatenate([st["mid", k] for k in range(TOK // ROWS)], axis=0)

        def widen(f):
            lanes = slice(f * CHUNK, (f + 1) * CHUNK)
            up_ = dot(st["mid"], wup[b, :, lanes]) + bup[pl.ds(b, 1), lanes]
            hid[:, lanes] = twice_gelu(up_).astype(BF16)

        def narrow(n):
            lanes = slice(n * 256, (n + 1) * 256)
            st["red", n] = dot(hid[...], wdown[b, :, lanes]) + 2.0 * bdown[pl.ds(b, 1), lanes]

        def finish(c):
            part = slice(c * ROWS, (c + 1) * ROWS)
            red = jnp.concatenate([st["red", 0][part], st["red", 1][part]], axis=1)
            y = st["mid", c].astype(F32) + layer_norm(red, gain[b, 1:2, :], shift[b, 1:2, :], 4.0 * NORM_EPS)
            keep = jnp.logical_or(mask[i, j] == 1, b == 1)
            y = jnp.where(keep, y, st["x"][part]).astype(BF16)
            per = TOK // 2 // ROWS
            buf[b + 1, cb + c // per, pl.ds(pl.multiple_of(start + c % per * ROWS, ROWS), ROWS), :] = y

        steps = {("merge", 0): merge}
        for c in range(TOK // ROWS):
            steps["norm", c] = functools.partial(norm, c)
            steps["finish", c] = functools.partial(finish, c)
        for f in range(FF // CHUNK):
            steps["widen", f] = functools.partial(widen, f)
        for n in range(2):
            steps["narrow", n] = functools.partial(narrow, n)
        return steps

    for c in loads[0][1:]:
        c.wait()
    for c in loads[1]:
        c.start()
    first, ahead = attention(jnp.int32(0)), attention(jnp.int32(1))
    for step in PROJECT:
        first[step]()
    first["fetch", 0]()
    for h in range(HEADS):
        for b in range(2):
            expand_bias(wscr, bias, b, h)
        first["head", h]()
        for step in SPREAD.get(h, ()):
            ahead[step]()

    def both(t, carry):
        @pl.when(t == nwin - 1)
        def _():
            for c in loads[1]:
                c.wait()

        if remote:
            @pl.when(t == nwin)
            def _():
                halo[0].wait_recv()

            @pl.when(t == nwin + 1)
            def _():
                halo[1].wait_recv()

            @pl.when(t == nwin + 2)
            def _():
                halo[2].wait_recv()
                halo[3].wait_recv()

        now, ahead, behind = attention(t), attention(jnp.minimum(t + 1, 2 * nwin - 1)), feed(t - 1)
        now["fetch", 0]()
        ahead["start", 0]()
        for h in range(HEADS):
            now["head", h]()
            for step in AFTER.get(h, ()):
                (behind if step in behind else ahead)[step]()

        if remote:
            @pl.when(t == 2)
            def _():
                pl.semaphore_wait(barrier, 6)
                halo[0].start()

            @pl.when(t == 3)
            def _():
                halo[1].start()
                halo[2].start()

            @pl.when(t == 5)
            def _():
                halo[3].start()

            for pos in range(nwin):
                n_ = ORDER[1][pos]
                if back[n_] and pos < nwin - 1:
                    @pl.when(t == nwin + pos + 1)
                    def _(n_=n_):
                        for c in back[n_]:
                            c.start()
        return carry

    lax.fori_loop(1, 2 * nwin, both, 0)
    last_steps = feed(jnp.int32(2 * nwin - 1))
    for step in LAST:
        last_steps[step]()
    inside, below = pl.ds(edge_rows, own - edge_rows), pl.ds(0, edge_rows)
    later = pl.ds(1, halves - 1)
    outs = [
        pltpu.make_async_copy(buf.at[2, later, inside], out.at[later, inside], out_sem.at[0]),
        pltpu.make_async_copy(buf.at[2, later, below], out.at[later, below], out_sem.at[1]),
        pltpu.make_async_copy(buf.at[2, 0, pl.ds(0, own)], out.at[0], out_sem.at[2]),
    ]
    outs[0].start()
    if remote:
        for c in halo:
            c.wait_send()
        for cs in back:
            for c in cs:
                c.wait()
    outs[1].start()
    outs[2].start()
    for c in outs:
        c.wait()


def assemble(halves_ref, out_ref):
    rows = out_ref.shape[0]
    for j in range(out_ref.shape[1] // WIN):
        parts = [halves_ref[2 * j + b].astype(F32).reshape(rows, HALF, DIM) for b in range(2)]
        out_ref[:, j * WIN : (j + 1) * WIN, :] = jnp.concatenate(parts, axis=1).astype(BF16)


def body(remote, *args):
    tokens = args[0]
    tile_rows, tile_cols = tokens.shape[0], tokens.shape[1]
    ww = tile_cols // WIN
    vmem = pl.BlockSpec(memory_space=pltpu.VMEM)
    smem = pl.BlockSpec(memory_space=pltpu.SMEM)
    anym = pl.BlockSpec(memory_space=pl.ANY)
    halves = 2 * ww
    encoded = pl.pallas_call(
        functools.partial(kernel, remote),
        out_shape=jax.ShapeDtypeStruct((halves, tile_rows * HALF, DIM), BF16),
        in_specs=[anym, smem, anym, vmem, anym, vmem, anym, vmem, anym, vmem, vmem, vmem, smem, vmem],
        out_specs=anym,
        scratch_shapes=[
            pltpu.VMEM(tokens.shape, BF16),
            pltpu.VMEM((2, DIM, 3 * DIM), BF16),
            pltpu.VMEM((2, DIM, DIM), BF16),
            pltpu.VMEM((2, DIM, FF), BF16),
            pltpu.VMEM((2, FF, DIM), BF16),
            pltpu.VMEM((3, 2 * ww + 1, (tile_rows + HALF) * HALF, DIM), BF16),
            pltpu.VMEM((2, HEADS, TOK, TOK), BF16),
            pltpu.VMEM((2 * HEADS, LANES_POS), F32),
            pltpu.VMEM((2, 3 * 256, 128), F32),
            pltpu.VMEM((TOK, 4 * TOK), BF16),
            pltpu.VMEM((4 * TOK, 256), BF16),
            pltpu.VMEM((TOK, DIM), BF16),
            pltpu.VMEM((TOK, FF), BF16),
            pltpu.VMEM((256, 256), BF16),
            pltpu.VMEM((4, WIN, 128), BF16),
            pltpu.VMEM((3, 2, TOK, 256), BF16),
            pltpu.VMEM((4, TOK, 128), BF16),
            pltpu.VMEM((4, TOK, 128), BF16),
            pltpu.SemaphoreType.DMA((9,)),
            pltpu.SemaphoreType.DMA((3,)),
            pltpu.SemaphoreType.DMA((10,)),
            pltpu.SemaphoreType.DMA((10,)),
        ],
        compiler_params=pltpu.CompilerParams(
            collective_id=0 if remote else None,
            has_side_effects=remote,
            vmem_limit_bytes=56 * 1024 * 1024,
        ),
    )(*args)
    return pl.pallas_call(
        assemble,
        grid=(tile_rows // OUT_ROWS,),
        out_shape=jax.ShapeDtypeStruct(tokens.shape, BF16),
        in_specs=[pl.BlockSpec((halves, OUT_ROWS * HALF, DIM), lambda i: (0, i, 0))],
        out_specs=pl.BlockSpec((OUT_ROWS, tile_cols, DIM), lambda i: (i, 0, 0)),
    )(encoded)


def solution(mesh):
    return jax.shard_map(
        functools.partial(body, True),
        mesh=mesh,
        in_specs=(P("row", "col", None), P("row", "col")) + (P(),) * 12,
        out_specs=P("row", "col", None),
        check_vma=False,
    )
```

```python
import functools

import jax
import jax.numpy as jnp
from jax import lax
from jax.experimental import pallas as pl
from jax.experimental.pallas import tpu as pltpu
from jax.sharding import PartitionSpec as P

DIM = 512
HEADS = 16
HEAD_DIM = 32
FF = 2048
WIN = 16
HALF = 8
SPAN = 31
POS = 961
TOK = WIN * WIN
NORM_EPS = 1e-05
LOG2E = 1.4426950408889634
LANES_POS = 1024
CHUNK = 256
ORDER = ((0, 3, 2, 5, 1, 4), (2, 5, 3, 4, 0, 1))
PROJECT = [("start", 0)] + [(p, g) for g in range(2) for p in ("q", "k", "v", "unit")]
LAST = (
    [("merge", 0)] + [("norm", c) for c in range(4)] + [("widen", f) for f in range(8)]
    + [("narrow", 0), ("narrow", 1)] + [("finish", c) for c in range(4)]
)
SPREAD = {
    1: [("start", 0), ("q", 0)], 3: [("k", 0)], 5: [("v", 0)], 7: [("unit", 0)], 9: [("q", 1)], 11: [("k", 1)], 13: [("v", 1)], 14: [("unit", 1)],
}
AFTER = {
    0: [("merge", 0), ("q", 0)],
    1: [("norm", 0), ("k", 0)],
    2: [("norm", 1), ("v", 0), ("unit", 0)],
    3: [("norm", 2), ("norm", 3), ("q", 1)],
    4: [("widen", 0), ("k", 1)],
    5: [("widen", 1)],
    6: [("widen", 2)],
    7: [("widen", 3)],
    8: [("widen", 4)],
    9: [("widen", 5)],
    10: [("widen", 6)],
    11: [("widen", 7)],
    12: [("narrow", 0)],
    13: [("narrow", 1), ("finish", 0)],
    14: [("finish", 1), ("finish", 2), ("v", 1)],
    15: [("finish", 3), ("unit", 1)],
}

GELU_POLY = (
    0.7978275766755302,
    0.036469930643555554,
    -0.00012547612359992849,
    -3.0467214006275725e-05,
    1.1126326266502673e-06,
)
PENALTY = -30000.0
ROWS = 64
OUT_ROWS = 16

F32 = jnp.float32
BF16 = jnp.bfloat16
MESH = pl.DeviceIdType.MESH


def dot(a, b):
    return jnp.dot(a, b, preferred_element_type=F32)


def twice_gelu(x):
    v = x.astype(BF16)
    u = v * v
    p = jnp.asarray(GELU_POLY[-1], BF16)
    for c in GELU_POLY[-2::-1]:
        p = p * u + jnp.asarray(c, BF16)
    return v * (jnp.tanh(v * p) + jnp.asarray(1.0, BF16))


def layer_norm(v, g, s, eps):
    m = jnp.mean(v, axis=-1, keepdims=True)
    c = v - m
    var = jnp.mean(c * c, axis=-1, keepdims=True)
    return c * lax.rsqrt(var + eps) * g + s


def spread_table(table, tscr, wscr):
    tscr[...] = jnp.zeros_like(tscr)
    for b in range(2):
        tscr[b * HEADS : (b + 1) * HEADS, 0:POS] = jnp.exp2(table[b] * LOG2E)
    t = tscr[...]
    r = jnp.concatenate([pltpu.roll(t, LANES_POS - c, 1) if c else t for c in range(8)], axis=0).astype(BF16)
    rows = lax.broadcasted_iota(jnp.int32, (LANES_POS, 256), 0)
    lane = lax.broadcasted_iota(jnp.int32, (1, 256), 1)
    target = (30 - (lane >> 3)) * SPAN + 7 - (lane & 7)
    for d in range(3):
        pick = jnp.where(rows == target + 8 * d, 1.0, 0.0).astype(BF16)
        w = dot(r, pick)
        for half in range(2):
            wscr[half, d * 256 : (d + 1) * 256, :] = w[:, half * 128 : (half + 1) * 128]


def expand_bias(wscr, bias, b, h):
    lane = lax.broadcasted_iota(jnp.int32, (HALF, 128), 1)
    for d in range(3):
        rows8 = pl.ds(d * 256 + b * HEADS + h, 8, stride=32)
        w0, w1 = wscr[0, rows8, :], wscr[1, rows8, :]
        for rp in range(0, WIN, 2):
            pair = []
            for o in ((15 - rp) * 8, (14 - rp) * 8):
                pair.append(pltpu.roll(jnp.where(lane < o, w1, w0), 128 - o, 1) if o else w0)
            piece = jnp.concatenate(pair, axis=0).astype(BF16)
            for bp in range(2):
                bq = bp - (d - 1)
                if 0 <= bq < 2:
                    bias[b, h, bp * 128 + rp * 8 : bp * 128 + rp * 8 + 16, bq * 128 : bq * 128 + 128] = piece


def kernel(
    remote,
    tok_hbm, mask, wqkv_hbm, bqkv, wproj_hbm, bproj, wup_hbm, bup, wdown_hbm, bdown,
    gain, shift, lscale, table,
    out,
    tok, wqkv, wproj, wup, wdown, buf, bias, tscr, wscr, prob, vone, ctx, hid, same, hmask, unit_qkv, qlab, klab, load_sem, out_sem, send_sem, recv_sem,
):
    tile_rows, tile_cols = tok.shape[0], tok.shape[1]
    wh, ww = tile_rows // WIN, tile_cols // WIN
    nwin = wh * ww
    own = tile_rows * HALF
    edge_rows = HALF * HALF
    halves = 2 * ww

    loads = [[pltpu.make_async_copy(tok_hbm, tok, load_sem.at[0])], []]
    for b in range(2):
        for k, (src, dst) in enumerate(((wqkv_hbm, wqkv), (wproj_hbm, wproj), (wup_hbm, wup), (wdown_hbm, wdown))):
            loads[b].append(pltpu.make_async_copy(src.at[b], dst.at[b], load_sem.at[1 + 4 * b + k]))
    for c in loads[0]:
        c.start()

    if remote:
        row, col = lax.axis_index("row"), lax.axis_index("col")
        nrow, ncol = lax.axis_size("row"), lax.axis_size("col")
        up, down = lax.rem(row + nrow - 1, nrow), lax.rem(row + 1, nrow)
        left, right = lax.rem(col + ncol - 1, ncol), lax.rem(col + 1, ncol)
        barrier = pltpu.get_barrier_semaphore()
        for dev in ((up, col), (row, left), (up, left), (down, col), (row, right), (down, right)):
            pl.semaphore_signal(barrier, inc=1, device_id=dev, device_id_type=MESH)
        last_row = row == nrow - 1
        last_col = col == ncol - 1

        def copy(k, src, dst, dev):
            return pltpu.make_async_remote_copy(
                src_ref=src, dst_ref=dst, send_sem=send_sem.at[k], recv_sem=recv_sem.at[k],
                device_id=dev, device_id_type=MESH,
            )

        stage1, stage2 = buf.at[1], buf.at[2]
        inner = pl.ds(0, edge_rows)
        outer = pl.ds(own, edge_rows)
        def to_above(k, j):
            cols = pl.ds(2 * j, 2)
            return copy(k, stage1.at[cols, inner], stage1.at[cols, outer], (up, col))

        halo = [
            to_above(0, 0),
            to_above(1, 1),
            to_above(2, 2),
            copy(3, stage1.at[0, pl.ds(0, own)], stage1.at[halves, pl.ds(0, own)], (row, left)),
            copy(4, stage1.at[0, inner], stage1.at[halves, outer], (up, left)),
        ]
        back = [[] for _ in range(nwin)]
        k = 5
        for i in range(wh):
            for j in range(ww):
                n = i * ww + j
                low, right_edge = i == wh - 1, j == ww - 1
                start = edge_rows + i * TOK // 2
                size = TOK // 2 - (edge_rows if low else 0)
                if low:
                    cnt = 1 if right_edge else 2
                    cols = pl.ds(2 * j + 1, cnt)
                    back[n].append(copy(k, stage2.at[cols, outer], stage2.at[cols, inner], (down, col)))
                    k += 1
                if right_edge:
                    rows = pl.ds(start, size)
                    back[n].append(copy(k, stage2.at[halves, rows], stage2.at[0, rows], (row, right)))
                    k += 1
                if low and right_edge:
                    back[n].append(copy(k, stage2.at[halves, outer], stage2.at[0, inner], (down, right)))
                    k += 1
    else:
        last_row = last_col = jnp.bool_(False)

    loads[0][0].wait()
    for j in range(ww):
        t = tok[:, j * WIN : (j + 1) * WIN, :].astype(F32)
        for b in range(2):
            buf[0, 2 * j + b, 0:own, :] = t[:, b * HALF : (b + 1) * HALF, :].reshape(own, DIM).astype(BF16)

    spread_table(table, tscr, wscr)

    r256 = lax.broadcasted_iota(jnp.int32, (256, 256), 0)
    c256 = lax.broadcasted_iota(jnp.int32, (256, 256), 1)
    same[...] = jnp.where((r256 >> 5) == (c256 >> 5), 1.0, 0.0).astype(BF16)
    head_lane = lax.broadcasted_iota(jnp.int32, (WIN, 128), 1) >> 5
    for h in range(4):
        hmask[h] = jnp.where(head_lane == h, 1.0, 0.0).astype(BF16)
    token = lax.broadcasted_iota(jnp.int32, (TOK, 128), 0)
    lane128 = lax.broadcasted_iota(jnp.int32, (TOK, 128), 1)
    for case in range(4):
        label = ((token >> 6) & 1) * (case & 2) + (token >> 7) * (case & 1)
        qlab[case] = jnp.where(lane128 == label, 1.0, 0.0).astype(BF16)
        klab[case] = jnp.where(jnp.logical_or(lane128 == label, lane128 > 3), 0.0, PENALTY).astype(BF16)
    for h in range(4):
        vone[h * TOK : (h + 1) * TOK, 128:256] = jnp.where((lane128 >> 5) == h, 1.0, 0.0).astype(BF16)
    lane512 = lax.broadcasted_iota(jnp.int32, (1, DIM), 1)

    def place(w):
        b = w // nwin
        n = w % nwin
        idx = jnp.int32(0)
        for k in range(nwin):
            idx = idx + jnp.where(n == k, jnp.where(b == 0, ORDER[0][k], ORDER[1][k]), 0)
        i = idx // ww
        j = idx % ww
        cb = 2 * j + b
        start = pl.multiple_of(i * (TOK // 2) + b * edge_rows, edge_rows)
        return b, i, j, cb, start

    def load_x(b, cb, start):
        rows = pl.ds(start, TOK // 2)
        return jnp.concatenate([buf[b, cb, rows, :], buf[b, cb + 1, rows, :]], axis=0)

    def attention(w):
        b, i, j, cb, start = place(w)
        st = {}

        def begin():
            st["x"] = load_x(b, cb, start)
            sc = jnp.zeros((1, DIM), F32)
            for h in range(HEADS):
                sc = jnp.where((lane512 >> 5) == h, lscale[b, h] * LOG2E, sc)
            st["sc"] = sc

        def fetch():
            cut_row = jnp.logical_and(jnp.logical_and(last_row, b == 1), i == wh - 1)
            cut_col = jnp.logical_and(jnp.logical_and(last_col, b == 1), j == ww - 1)
            st["case"] = cut_row.astype(jnp.int32) * 2 + cut_col.astype(jnp.int32)
            for g in range(2):
                for n, name in enumerate(("qn", "kn", "vn")):
                    st[name, g] = unit_qkv[n, g]

        def project(part, g):
            lanes = slice(part * DIM + g * 256, part * DIM + (g + 1) * 256)
            r = dot(st["x"], wqkv[b, :, lanes]) + bqkv[pl.ds(b, 1), lanes]
            if part == 2:
                unit_qkv[2, g] = r.astype(BF16)
            else:
                st[part, g] = r

        def unit(g):
            lanes = slice(g * 256, (g + 1) * 256)
            qg, kg = st[0, g], st[1, g]
            q2 = dot((qg * qg).astype(BF16), same[...])
            k2 = dot((kg * kg).astype(BF16), same[...])
            unit_qkv[0, g] = (qg * (lax.rsqrt(jnp.maximum(q2, 1.0)) * st["sc"][:, lanes])).astype(BF16)
            unit_qkv[1, g] = (kg * lax.rsqrt(jnp.maximum(k2, 1.0))).astype(BF16)

        def head(h):
            h4, g = h % 4, h // 8
            here = slice((h - h4) % 8 * HEAD_DIM, (h - h4) % 8 * HEAD_DIM + 128)
            only = hmask[h4][None]
            vg = st["vn", g][:, here].reshape(WIN, WIN, 128)
            vone[h4 * TOK : (h4 + 1) * TOK, 0:128] = (vg * only).reshape(TOK, 128)
            qm = (st["qn", g][:, here].reshape(WIN, WIN, 128) * only).reshape(TOK, 128)
            s = lax.dot_general(
                jnp.concatenate([qm, qlab[st["case"]]], axis=1),
                jnp.concatenate([st["kn", g][:, here], klab[st["case"]]], axis=1),
                (((1,), (1,)), ((), ())), preferred_element_type=F32,
            )
            prob[:, h4 * TOK : (h4 + 1) * TOK] = jnp.exp2(s).astype(BF16) * bias[b, h]
            if h4 == 3:
                o = dot(prob[...], vone[...])
                v0 = (h - 3) * HEAD_DIM
                ctx[:, v0 : v0 + 128] = (o[:, 0:128] * pl.reciprocal(o[:, 128:256], approx=True)).astype(BF16)

        steps = {("start", 0): begin, ("fetch", 0): fetch}
        for g in range(2):
            steps["unit", g] = functools.partial(unit, g)
            for part in range(3):
                steps["qkv"[part], g] = functools.partial(project, part, g)
        for h in range(HEADS):
            steps["head", h] = functools.partial(head, h)
        return steps

    def feed(w):
        b, i, j, cb, start = place(w)
        st = {}

        def merge():
            st["x"] = load_x(b, cb, start).astype(F32)
            st["att"] = dot(ctx[...], wproj[b]) + bproj[pl.ds(b, 1), :]

        def norm(c):
            part = slice(c * ROWS, (c + 1) * ROWS)
            mid = st["x"][part] + layer_norm(st["att"][part], gain[b, 0:1, :], shift[b, 0:1, :], NORM_EPS)
            st["mid", c] = mid.astype(BF16)
            if c == TOK // ROWS - 1:
                st["mid"] = jnp.concatenate([st["mid", k] for k in range(TOK // ROWS)], axis=0)

        def widen(f):
            lanes = slice(f * CHUNK, (f + 1) * CHUNK)
            up_ = dot(st["mid"], wup[b, :, lanes]) + bup[pl.ds(b, 1), lanes]
            hid[:, lanes] = twice_gelu(up_).astype(BF16)

        def narrow(n):
            lanes = slice(n * 256, (n + 1) * 256)
            st["red", n] = dot(hid[...], wdown[b, :, lanes]) + 2.0 * bdown[pl.ds(b, 1), lanes]

        def finish(c):
            part = slice(c * ROWS, (c + 1) * ROWS)
            red = jnp.concatenate([st["red", 0][part], st["red", 1][part]], axis=1)
            y = st["mid", c].astype(F32) + layer_norm(red, gain[b, 1:2, :], shift[b, 1:2, :], 4.0 * NORM_EPS)
            keep = jnp.logical_or(mask[i, j] == 1, b == 1)
            y = jnp.where(keep, y, st["x"][part]).astype(BF16)
            per = TOK // 2 // ROWS
            buf[b + 1, cb + c // per, pl.ds(pl.multiple_of(start + c % per * ROWS, ROWS), ROWS), :] = y

        steps = {("merge", 0): merge}
        for c in range(TOK // ROWS):
            steps["norm", c] = functools.partial(norm, c)
            steps["finish", c] = functools.partial(finish, c)
        for f in range(FF // CHUNK):
            steps["widen", f] = functools.partial(widen, f)
        for n in range(2):
            steps["narrow", n] = functools.partial(narrow, n)
        return steps

    for c in loads[0][1:]:
        c.wait()
    for c in loads[1]:
        c.start()
    first, ahead = attention(jnp.int32(0)), attention(jnp.int32(1))
    for step in PROJECT:
        first[step]()
    first["fetch", 0]()
    for h in range(HEADS):
        for b in range(2):
            expand_bias(wscr, bias, b, h)
        first["head", h]()
        for step in SPREAD.get(h, ()):
            ahead[step]()

    def both(t, carry):
        @pl.when(t == nwin - 1)
        def _():
            for c in loads[1]:
                c.wait()

        if remote:
            @pl.when(t == nwin - 1)
            def _():
                halo[3].wait_recv()

            @pl.when(t == nwin)
            def _():
                halo[2].wait_recv()
                halo[4].wait_recv()

            @pl.when(t == nwin + 1)
            def _():
                halo[0].wait_recv()
                halo[1].wait_recv()

        now, ahead, behind = attention(t), attention(jnp.minimum(t + 1, 2 * nwin - 1)), feed(t - 1)
        now["fetch", 0]()
        ahead["start", 0]()
        for h in range(HEADS):
            now["head", h]()
            for step in AFTER.get(h, ()):
                (behind if step in behind else ahead)[step]()

        if remote:
            @pl.when(t == 2)
            def _():
                pl.semaphore_wait(barrier, 6)
                for k in (3, 4, 0):
                    halo[k].start()

            @pl.when(t == 3)
            def _():
                halo[2].start()

            @pl.when(t == 5)
            def _():
                halo[1].start()

            for pos in range(nwin):
                n_ = ORDER[1][pos]
                if back[n_] and pos < nwin - 1:
                    @pl.when(t == nwin + pos + 1)
                    def _(n_=n_):
                        for c in back[n_]:
                            c.start()
        return carry

    lax.fori_loop(1, 2 * nwin, both, 0)
    last_steps = feed(jnp.int32(2 * nwin - 1))
    for step in LAST:
        last_steps[step]()
    inside, below = pl.ds(edge_rows, own - edge_rows), pl.ds(0, edge_rows)
    later = pl.ds(1, halves - 1)
    outs = [
        pltpu.make_async_copy(buf.at[2, later, inside], out.at[later, inside], out_sem.at[0]),
        pltpu.make_async_copy(buf.at[2, later, below], out.at[later, below], out_sem.at[1]),
        pltpu.make_async_copy(buf.at[2, 0, pl.ds(0, own)], out.at[0], out_sem.at[2]),
    ]
    outs[0].start()
    if remote:
        for c in halo:
            c.wait_send()
        for cs in back:
            for c in cs:
                c.wait()
    outs[1].start()
    outs[2].start()
    for c in outs:
        c.wait()


def assemble(halves_ref, out_ref):
    rows = out_ref.shape[0]
    for j in range(out_ref.shape[1] // WIN):
        parts = [halves_ref[2 * j + b].astype(F32).reshape(rows, HALF, DIM) for b in range(2)]
        out_ref[:, j * WIN : (j + 1) * WIN, :] = jnp.concatenate(parts, axis=1).astype(BF16)


def body(remote, *args):
    tokens = args[0]
    tile_rows, tile_cols = tokens.shape[0], tokens.shape[1]
    ww = tile_cols // WIN
    vmem = pl.BlockSpec(memory_space=pltpu.VMEM)
    smem = pl.BlockSpec(memory_space=pltpu.SMEM)
    anym = pl.BlockSpec(memory_space=pl.ANY)
    halves = 2 * ww
    encoded = pl.pallas_call(
        functools.partial(kernel, remote),
        out_shape=jax.ShapeDtypeStruct((halves, tile_rows * HALF, DIM), BF16),
        in_specs=[anym, smem, anym, vmem, anym, vmem, anym, vmem, anym, vmem, vmem, vmem, smem, vmem],
        out_specs=anym,
        scratch_shapes=[
            pltpu.VMEM(tokens.shape, BF16),
            pltpu.VMEM((2, DIM, 3 * DIM), BF16),
            pltpu.VMEM((2, DIM, DIM), BF16),
            pltpu.VMEM((2, DIM, FF), BF16),
            pltpu.VMEM((2, FF, DIM), BF16),
            pltpu.VMEM((3, 2 * ww + 1, (tile_rows + HALF) * HALF, DIM), BF16),
            pltpu.VMEM((2, HEADS, TOK, TOK), BF16),
            pltpu.VMEM((2 * HEADS, LANES_POS), F32),
            pltpu.VMEM((2, 3 * 256, 128), F32),
            pltpu.VMEM((TOK, 4 * TOK), BF16),
            pltpu.VMEM((4 * TOK, 256), BF16),
            pltpu.VMEM((TOK, DIM), BF16),
            pltpu.VMEM((TOK, FF), BF16),
            pltpu.VMEM((256, 256), BF16),
            pltpu.VMEM((4, WIN, 128), BF16),
            pltpu.VMEM((3, 2, TOK, 256), BF16),
            pltpu.VMEM((4, TOK, 128), BF16),
            pltpu.VMEM((4, TOK, 128), BF16),
            pltpu.SemaphoreType.DMA((9,)),
            pltpu.SemaphoreType.DMA((3,)),
            pltpu.SemaphoreType.DMA((11,)),
            pltpu.SemaphoreType.DMA((11,)),
        ],
        compiler_params=pltpu.CompilerParams(
            collective_id=0 if remote else None,
            has_side_effects=remote,
            vmem_limit_bytes=56 * 1024 * 1024,
        ),
    )(*args)
    return pl.pallas_call(
        assemble,
        grid=(tile_rows // OUT_ROWS,),
        out_shape=jax.ShapeDtypeStruct(tokens.shape, BF16),
        in_specs=[pl.BlockSpec((halves, OUT_ROWS * HALF, DIM), lambda i: (0, i, 0))],
        out_specs=pl.BlockSpec((OUT_ROWS, tile_cols, DIM), lambda i: (i, 0, 0)),
    )(encoded)


def solution(mesh):
    return jax.shard_map(
        functools.partial(body, True),
        mesh=mesh,
        in_specs=(P("row", "col", None), P("row", "col")) + (P(),) * 12,
        out_specs=P("row", "col", None),
        check_vma=False,
    )
```

```python
import functools

import jax
import jax.numpy as jnp
from jax import lax
from jax.experimental import pallas as pl
from jax.experimental.pallas import tpu as pltpu
from jax.sharding import PartitionSpec as P

DIM = 512
HEADS = 16
HEAD_DIM = 32
FF = 2048
WIN = 16
HALF = 8
SPAN = 31
POS = 961
TOK = WIN * WIN
NORM_EPS = 1e-05
LOG2E = 1.4426950408889634
LANES_POS = 1024
CHUNK = 256
ORDER = ((0, 3, 2, 5, 1, 4), (2, 5, 3, 4, 0, 1))
PROJECT = [("start", 0)] + [(p, g) for g in range(2) for p in ("q", "k", "v", "unit")]
LAST = (
    [("merge", 0)] + [("norm", c) for c in range(4)] + [("widen", f) for f in range(8)]
    + [("narrow", 0), ("narrow", 1)] + [("finish", c) for c in range(4)]
)
SPREAD = {
    1: [("start", 0), ("q", 0)], 3: [("k", 0)], 5: [("v", 0)], 7: [("unit", 0)], 9: [("q", 1)], 11: [("k", 1)], 13: [("v", 1)], 14: [("unit", 1)],
}
AFTER = {
    0: [("merge", 0), ("q", 0)],
    1: [("norm", 0), ("k", 0)],
    2: [("norm", 1), ("v", 0), ("unit", 0)],
    3: [("norm", 2), ("norm", 3), ("q", 1)],
    4: [("widen", 0), ("k", 1)],
    5: [("widen", 1)],
    6: [("widen", 2)],
    7: [("widen", 3)],
    8: [("widen", 4)],
    9: [("widen", 5)],
    10: [("widen", 6)],
    11: [("widen", 7)],
    12: [("narrow", 0)],
    13: [("narrow", 1), ("finish", 0)],
    14: [("finish", 1), ("finish", 2), ("v", 1)],
    15: [("finish", 3), ("unit", 1)],
}

GELU_POLY = (
    0.7978275766755302,
    0.036469930643555554,
    -0.00012547612359992849,
    -3.0467214006275725e-05,
    1.1126326266502673e-06,
)
PENALTY = -30000.0
ROWS = 64
OUT_ROWS = 16

F32 = jnp.float32
BF16 = jnp.bfloat16
MESH = pl.DeviceIdType.MESH


def dot(a, b):
    return jnp.dot(a, b, preferred_element_type=F32)


def twice_gelu(x):
    v = x.astype(BF16)
    u = v * v
    p = jnp.asarray(GELU_POLY[-1], BF16)
    for c in GELU_POLY[-2::-1]:
        p = p * u + jnp.asarray(c, BF16)
    return v * (jnp.tanh(v * p) + jnp.asarray(1.0, BF16))


def layer_norm(v, g, s, eps):
    m = jnp.mean(v, axis=-1, keepdims=True)
    c = v - m
    var = jnp.mean(c * c, axis=-1, keepdims=True)
    return c * lax.rsqrt(var + eps) * g + s


def spread_table(table, tscr, wscr):
    tscr[...] = jnp.zeros_like(tscr)
    for b in range(2):
        tscr[b * HEADS : (b + 1) * HEADS, 0:POS] = jnp.exp2(table[b] * LOG2E)
    t = tscr[...]
    r = jnp.concatenate([pltpu.roll(t, LANES_POS - c, 1) if c else t for c in range(8)], axis=0).astype(BF16)
    rows = lax.broadcasted_iota(jnp.int32, (LANES_POS, 256), 0)
    lane = lax.broadcasted_iota(jnp.int32, (1, 256), 1)
    target = (30 - (lane >> 3)) * SPAN + 7 - (lane & 7)
    for d in range(3):
        pick = jnp.where(rows == target + 8 * d, 1.0, 0.0).astype(BF16)
        w = dot(r, pick)
        for half in range(2):
            wscr[half, d * 256 : (d + 1) * 256, :] = w[:, half * 128 : (half + 1) * 128]


def expand_bias(wscr, bias, b, h):
    lane = lax.broadcasted_iota(jnp.int32, (HALF, 128), 1)
    for d in range(3):
        rows8 = pl.ds(d * 256 + b * HEADS + h, 8, stride=32)
        w0, w1 = wscr[0, rows8, :], wscr[1, rows8, :]
        for rp in range(0, WIN, 2):
            pair = []
            for o in ((15 - rp) * 8, (14 - rp) * 8):
                pair.append(pltpu.roll(jnp.where(lane < o, w1, w0), 128 - o, 1) if o else w0)
            piece = jnp.concatenate(pair, axis=0).astype(BF16)
            for bp in range(2):
                bq = bp - (d - 1)
                if 0 <= bq < 2:
                    bias[b, h, bp * 128 + rp * 8 : bp * 128 + rp * 8 + 16, bq * 128 : bq * 128 + 128] = piece


def kernel(
    remote,
    tok_hbm, mask, wqkv_hbm, bqkv, wproj_hbm, bproj, wup_hbm, bup, wdown_hbm, bdown,
    gain, shift, lscale, table,
    out,
    tok, wqkv, wproj, wup, wdown, buf, bias, tscr, wscr, prob, vone, ctx, hid, same, hmask, unit_qkv, qlab, klab, load_sem, out_sem, send_sem, recv_sem,
):
    tile_rows, tile_cols = tok.shape[0], tok.shape[1]
    wh, ww = tile_rows // WIN, tile_cols // WIN
    nwin = wh * ww
    own = tile_rows * HALF
    edge_rows = HALF * HALF
    halves = 2 * ww

    loads = [[pltpu.make_async_copy(tok_hbm, tok, load_sem.at[0])], []]
    for b in range(2):
        for k, (src, dst) in enumerate(((wqkv_hbm, wqkv), (wproj_hbm, wproj), (wup_hbm, wup), (wdown_hbm, wdown))):
            loads[b].append(pltpu.make_async_copy(src.at[b], dst.at[b], load_sem.at[1 + 4 * b + k]))
    for c in loads[0]:
        c.start()

    if remote:
        row, col = lax.axis_index("row"), lax.axis_index("col")
        nrow, ncol = lax.axis_size("row"), lax.axis_size("col")
        up, down = lax.rem(row + nrow - 1, nrow), lax.rem(row + 1, nrow)
        left, right = lax.rem(col + ncol - 1, ncol), lax.rem(col + 1, ncol)
        barrier = pltpu.get_barrier_semaphore()
        for dev in ((up, col), (row, left), (up, left), (down, col), (row, right), (down, right)):
            pl.semaphore_signal(barrier, inc=1, device_id=dev, device_id_type=MESH)
        last_row = row == nrow - 1
        last_col = col == ncol - 1

        def copy(k, src, dst, dev):
            return pltpu.make_async_remote_copy(
                src_ref=src, dst_ref=dst, send_sem=send_sem.at[k], recv_sem=recv_sem.at[k],
                device_id=dev, device_id_type=MESH,
            )

        stage1, stage2 = buf.at[1], buf.at[2]
        inner = pl.ds(0, edge_rows)
        outer = pl.ds(own, edge_rows)
        def to_above(k, j):
            cols = pl.ds(2 * j, 2)
            return copy(k, stage1.at[cols, inner], stage1.at[cols, outer], (up, col))

        halo = [
            to_above(0, 0),
            to_above(1, 1),
            to_above(2, 2),
            copy(3, stage1.at[0, pl.ds(0, own)], stage1.at[halves, pl.ds(0, own)], (row, left)),
            copy(4, stage1.at[0, inner], stage1.at[halves, outer], (up, left)),
        ]
        back = [[] for _ in range(nwin)]
        k = 5
        for i in range(wh):
            for j in range(ww):
                n = i * ww + j
                low, right_edge = i == wh - 1, j == ww - 1
                start = edge_rows + i * TOK // 2
                size = TOK // 2 - (edge_rows if low else 0)
                if low:
                    cnt = 1 if right_edge else 2
                    cols = pl.ds(2 * j + 1, cnt)
                    back[n].append(copy(k, stage2.at[cols, outer], stage2.at[cols, inner], (down, col)))
                    k += 1
                if right_edge:
                    rows = pl.ds(start, size)
                    back[n].append(copy(k, stage2.at[halves, rows], stage2.at[0, rows], (row, right)))
                    k += 1
                if low and right_edge:
                    back[n].append(copy(k, stage2.at[halves, outer], stage2.at[0, inner], (down, right)))
                    k += 1
    else:
        last_row = last_col = jnp.bool_(False)

    loads[0][0].wait()
    for j in range(ww):
        t = tok[:, j * WIN : (j + 1) * WIN, :].astype(F32)
        for b in range(2):
            buf[0, 2 * j + b, 0:own, :] = t[:, b * HALF : (b + 1) * HALF, :].reshape(own, DIM).astype(BF16)

    spread_table(table, tscr, wscr)

    r256 = lax.broadcasted_iota(jnp.int32, (256, 256), 0)
    c256 = lax.broadcasted_iota(jnp.int32, (256, 256), 1)
    same[...] = jnp.where((r256 >> 5) == (c256 >> 5), 1.0, 0.0).astype(BF16)
    head_lane = lax.broadcasted_iota(jnp.int32, (WIN, 128), 1) >> 5
    for h in range(4):
        hmask[h] = jnp.where(head_lane == h, 1.0, 0.0).astype(BF16)
    token = lax.broadcasted_iota(jnp.int32, (TOK, 128), 0)
    lane128 = lax.broadcasted_iota(jnp.int32, (TOK, 128), 1)
    for case in range(4):
        label = ((token >> 6) & 1) * (case & 2) + (token >> 7) * (case & 1)
        qlab[case] = jnp.where(lane128 == label, 1.0, 0.0).astype(BF16)
        klab[case] = jnp.where(jnp.logical_or(lane128 == label, lane128 > 3), 0.0, PENALTY).astype(BF16)
    for h in range(4):
        vone[h * TOK : (h + 1) * TOK, 128:256] = jnp.where((lane128 >> 5) == h, 1.0, 0.0).astype(BF16)
    lane512 = lax.broadcasted_iota(jnp.int32, (1, DIM), 1)

    def place(w):
        b = w // nwin
        n = w % nwin
        idx = jnp.int32(0)
        for k in range(nwin):
            idx = idx + jnp.where(n == k, jnp.where(b == 0, ORDER[0][k], ORDER[1][k]), 0)
        i = idx // ww
        j = idx % ww
        cb = 2 * j + b
        start = pl.multiple_of(i * (TOK // 2) + b * edge_rows, edge_rows)
        return b, i, j, cb, start

    def load_x(b, cb, start):
        rows = pl.ds(start, TOK // 2)
        return jnp.concatenate([buf[b, cb, rows, :], buf[b, cb + 1, rows, :]], axis=0)

    def attention(w):
        b, i, j, cb, start = place(w)
        st = {}

        def begin():
            st["x"] = load_x(b, cb, start)
            sc = jnp.zeros((1, DIM), F32)
            for h in range(HEADS):
                sc = jnp.where((lane512 >> 5) == h, lscale[b, h] * LOG2E, sc)
            st["sc"] = sc

        def fetch():
            cut_row = jnp.logical_and(jnp.logical_and(last_row, b == 1), i == wh - 1)
            cut_col = jnp.logical_and(jnp.logical_and(last_col, b == 1), j == ww - 1)
            st["case"] = cut_row.astype(jnp.int32) * 2 + cut_col.astype(jnp.int32)
            for g in range(2):
                for n, name in enumerate(("qn", "kn", "vn")):
                    st[name, g] = unit_qkv[n, g]

        def project(part, g):
            lanes = slice(part * DIM + g * 256, part * DIM + (g + 1) * 256)
            r = dot(st["x"], wqkv[b, :, lanes]) + bqkv[pl.ds(b, 1), lanes]
            if part == 2:
                unit_qkv[2, g] = r.astype(BF16)
            else:
                st[part, g] = r

        def unit(g):
            lanes = slice(g * 256, (g + 1) * 256)
            qg, kg = st[0, g], st[1, g]
            q2 = dot((qg * qg).astype(BF16), same[...])
            k2 = dot((kg * kg).astype(BF16), same[...])
            unit_qkv[0, g] = (qg * (lax.rsqrt(jnp.maximum(q2, 1.0)) * st["sc"][:, lanes])).astype(BF16)
            unit_qkv[1, g] = (kg * lax.rsqrt(jnp.maximum(k2, 1.0))).astype(BF16)

        def head(h):
            h4, g = h % 4, h // 8
            here = slice((h - h4) % 8 * HEAD_DIM, (h - h4) % 8 * HEAD_DIM + 128)
            only = hmask[h4][None]
            vg = st["vn", g][:, here].reshape(WIN, WIN, 128)
            vone[h4 * TOK : (h4 + 1) * TOK, 0:128] = (vg * only).reshape(TOK, 128)
            qm = (st["qn", g][:, here].reshape(WIN, WIN, 128) * only).reshape(TOK, 128)
            s = lax.dot_general(
                jnp.concatenate([qm, qlab[st["case"]]], axis=1),
                jnp.concatenate([st["kn", g][:, here], klab[st["case"]]], axis=1),
                (((1,), (1,)), ((), ())), preferred_element_type=F32,
            )
            prob[:, h4 * TOK : (h4 + 1) * TOK] = jnp.exp2(s).astype(BF16) * bias[b, h]
            if h4 == 3:
                o = dot(prob[...], vone[...])
                v0 = (h - 3) * HEAD_DIM
                ctx[:, v0 : v0 + 128] = (o[:, 0:128] * pl.reciprocal(o[:, 128:256], approx=True)).astype(BF16)

        steps = {("start", 0): begin, ("fetch", 0): fetch}
        for g in range(2):
            steps["unit", g] = functools.partial(unit, g)
            for part in range(3):
                steps["qkv"[part], g] = functools.partial(project, part, g)
        for h in range(HEADS):
            steps["head", h] = functools.partial(head, h)
        return steps

    def feed(w):
        b, i, j, cb, start = place(w)
        st = {}

        def merge():
            st["x"] = load_x(b, cb, start).astype(F32)
            st["att"] = dot(ctx[...], wproj[b]) + bproj[pl.ds(b, 1), :]

        def norm(c):
            part = slice(c * ROWS, (c + 1) * ROWS)
            mid = st["x"][part] + layer_norm(st["att"][part], gain[b, 0:1, :], shift[b, 0:1, :], NORM_EPS)
            st["mid", c] = mid.astype(BF16)
            if c == TOK // ROWS - 1:
                st["mid"] = jnp.concatenate([st["mid", k] for k in range(TOK // ROWS)], axis=0)

        def widen(f):
            lanes = slice(f * CHUNK, (f + 1) * CHUNK)
            up_ = dot(st["mid"], wup[b, :, lanes]) + bup[pl.ds(b, 1), lanes]
            hid[:, lanes] = twice_gelu(up_).astype(BF16)

        def narrow(n):
            lanes = slice(n * 256, (n + 1) * 256)
            st["red", n] = dot(hid[...], wdown[b, :, lanes]) + 2.0 * bdown[pl.ds(b, 1), lanes]

        def finish(c):
            part = slice(c * ROWS, (c + 1) * ROWS)
            red = jnp.concatenate([st["red", 0][part], st["red", 1][part]], axis=1)
            y = st["mid", c].astype(F32) + layer_norm(red, gain[b, 1:2, :], shift[b, 1:2, :], 4.0 * NORM_EPS)
            keep = jnp.logical_or(mask[i, j] == 1, b == 1)
            y = jnp.where(keep, y, st["x"][part]).astype(BF16)
            per = TOK // 2 // ROWS
            buf[b + 1, cb + c // per, pl.ds(pl.multiple_of(start + c % per * ROWS, ROWS), ROWS), :] = y

        steps = {("merge", 0): merge}
        for c in range(TOK // ROWS):
            steps["norm", c] = functools.partial(norm, c)
            steps["finish", c] = functools.partial(finish, c)
        for f in range(FF // CHUNK):
            steps["widen", f] = functools.partial(widen, f)
        for n in range(2):
            steps["narrow", n] = functools.partial(narrow, n)
        return steps

    for c in loads[0][1:]:
        c.wait()
    for c in loads[1]:
        c.start()
    first, ahead = attention(jnp.int32(0)), attention(jnp.int32(1))
    for step in PROJECT:
        first[step]()
    first["fetch", 0]()
    for h in range(HEADS):
        for b in range(2):
            expand_bias(wscr, bias, b, h)
        first["head", h]()
        for step in SPREAD.get(h, ()):
            ahead[step]()

    def both(t, carry):
        @pl.when(t == nwin - 1)
        def _():
            for c in loads[1]:
                c.wait()

        if remote:
            @pl.when(t == nwin - 1)
            def _():
                halo[3].wait_recv()

            @pl.when(t == nwin)
            def _():
                halo[2].wait_recv()
                halo[4].wait_recv()

            @pl.when(t == nwin + 1)
            def _():
                halo[0].wait_recv()
                halo[1].wait_recv()

        now, ahead, behind = attention(t), attention(t + 1), feed(t - 1)
        now["fetch", 0]()
        ahead["start", 0]()
        for h in range(HEADS):
            now["head", h]()
            for step in AFTER.get(h, ()):
                (behind if step in behind else ahead)[step]()

        if remote:
            @pl.when(t == 2)
            def _():
                pl.semaphore_wait(barrier, 6)
                for k in (3, 4, 0):
                    halo[k].start()

            @pl.when(t == 3)
            def _():
                halo[2].start()

            @pl.when(t == 5)
            def _():
                halo[1].start()

            for pos in range(nwin):
                n_ = ORDER[1][pos]
                if back[n_] and pos < nwin - 1:
                    @pl.when(t == nwin + pos + 1)
                    def _(n_=n_):
                        for c in back[n_]:
                            c.start()
        return carry

    lax.fori_loop(1, 2 * nwin - 1, both, 0)
    now, behind, last = attention(jnp.int32(2 * nwin - 1)), feed(jnp.int32(2 * nwin - 2)), feed(jnp.int32(2 * nwin - 1))
    now["fetch", 0]()
    for h in range(HEADS):
        now["head", h]()
        for step in AFTER.get(h, ()):
            if step in behind:
                behind[step]()

    column = 2 * (ORDER[1][-1] % ww) + 1
    inside, below = pl.ds(edge_rows, own - edge_rows), pl.ds(0, edge_rows)
    window_rows = pl.ds(edge_rows, TOK // 2)
    under = pl.ds(edge_rows + TOK // 2, own - edge_rows - TOK // 2)
    here = pl.ds(column, 2)
    places = (
        (pl.ds(1, column - 1), inside), (pl.ds(column + 2, halves - column - 2), inside), (here, under),
        (here, window_rows), (pl.ds(1, halves - 1), below), (pl.ds(0, 1), pl.ds(0, own)),
    )
    outs = [
        pltpu.make_async_copy(buf.at[2, cols, rows], out.at[cols, rows], out_sem.at[k])
        for k, (cols, rows) in enumerate(places)
    ]
    for c in outs[:3]:
        c.start()
    for step in LAST:
        last[step]()
    outs[3].start()
    if remote:
        for c in halo:
            c.wait_send()
        for cs in back:
            for c in cs:
                c.wait()
    for c in outs[4:]:
        c.start()
    for c in outs:
        c.wait()


def assemble(halves_ref, out_ref):
    rows = out_ref.shape[0]
    for j in range(out_ref.shape[1] // WIN):
        parts = [halves_ref[2 * j + b].astype(F32).reshape(rows, HALF, DIM) for b in range(2)]
        out_ref[:, j * WIN : (j + 1) * WIN, :] = jnp.concatenate(parts, axis=1).astype(BF16)


def body(remote, *args):
    tokens = args[0]
    tile_rows, tile_cols = tokens.shape[0], tokens.shape[1]
    ww = tile_cols // WIN
    vmem = pl.BlockSpec(memory_space=pltpu.VMEM)
    smem = pl.BlockSpec(memory_space=pltpu.SMEM)
    anym = pl.BlockSpec(memory_space=pl.ANY)
    halves = 2 * ww
    encoded = pl.pallas_call(
        functools.partial(kernel, remote),
        out_shape=jax.ShapeDtypeStruct((halves, tile_rows * HALF, DIM), BF16),
        in_specs=[anym, smem, anym, vmem, anym, vmem, anym, vmem, anym, vmem, vmem, vmem, smem, vmem],
        out_specs=anym,
        scratch_shapes=[
            pltpu.VMEM(tokens.shape, BF16),
            pltpu.VMEM((2, DIM, 3 * DIM), BF16),
            pltpu.VMEM((2, DIM, DIM), BF16),
            pltpu.VMEM((2, DIM, FF), BF16),
            pltpu.VMEM((2, FF, DIM), BF16),
            pltpu.VMEM((3, 2 * ww + 1, (tile_rows + HALF) * HALF, DIM), BF16),
            pltpu.VMEM((2, HEADS, TOK, TOK), BF16),
            pltpu.VMEM((2 * HEADS, LANES_POS), F32),
            pltpu.VMEM((2, 3 * 256, 128), F32),
            pltpu.VMEM((TOK, 4 * TOK), BF16),
            pltpu.VMEM((4 * TOK, 256), BF16),
            pltpu.VMEM((TOK, DIM), BF16),
            pltpu.VMEM((TOK, FF), BF16),
            pltpu.VMEM((256, 256), BF16),
            pltpu.VMEM((4, WIN, 128), BF16),
            pltpu.VMEM((3, 2, TOK, 256), BF16),
            pltpu.VMEM((4, TOK, 128), BF16),
            pltpu.VMEM((4, TOK, 128), BF16),
            pltpu.SemaphoreType.DMA((9,)),
            pltpu.SemaphoreType.DMA((6,)),
            pltpu.SemaphoreType.DMA((11,)),
            pltpu.SemaphoreType.DMA((11,)),
        ],
        compiler_params=pltpu.CompilerParams(
            collective_id=0 if remote else None,
            has_side_effects=remote,
            vmem_limit_bytes=56 * 1024 * 1024,
        ),
    )(*args)
    return pl.pallas_call(
        assemble,
        grid=(tile_rows // OUT_ROWS,),
        out_shape=jax.ShapeDtypeStruct(tokens.shape, BF16),
        in_specs=[pl.BlockSpec((halves, OUT_ROWS * HALF, DIM), lambda i: (0, i, 0))],
        out_specs=pl.BlockSpec((OUT_ROWS, tile_cols, DIM), lambda i: (i, 0, 0)),
    )(encoded)


def solution(mesh):
    return jax.shard_map(
        functools.partial(body, True),
        mesh=mesh,
        in_specs=(P("row", "col", None), P("row", "col")) + (P(),) * 12,
        out_specs=P("row", "col", None),
        check_vma=False,
    )
```
